32 devices in a mesh: worker: 2 (over core), fsdp: 16 (over z, y, x).
Axes of the slice: x: 2, y: 2, z: 4, core: 2. Of those that a mesh axis runs over, the one named last changes fastest.
Arguments:
- features: bfloat16 [6144, 8192], P(('worker', 'fsdp')), may hold values from -6 to 6
- value_cotangent: bfloat16 [6144, 512], P(('worker', 'fsdp')), may hold values from -6 to 6
- value_weight: float32 [2, 8192, 512], P('worker', 'fsdp'), may hold values from -0.25 to 0.25
- first_moment: float32 [2, 8192, 512], P('worker', 'fsdp'), may hold values from -48 to 48
- second_moment: float32 [2, 8192, 512], P('worker', 'fsdp'), may hold values from 1000 to 10000
- fragment_local: float32 [2, 8192, 512], P('worker', 'fsdp'), may hold values from -6 to 6
- fragment_anchor: float32 [8192, 512], P('fsdp'), may hold values from -6 to 6
- outer_momentum: float32 [8192, 512], P('fsdp'), may hold values from -3 to 3
Outputs:
- feature_grad: float32 [6144, 8192], P(('worker', 'fsdp'))
- new_weight: float32 [2, 8192, 512], P('worker', 'fsdp')
- new_first: float32 [2, 8192, 512], P('worker', 'fsdp')
- new_second: float32 [2, 8192, 512], P('worker', 'fsdp')
- new_anchor: float32 [8192, 512], P('fsdp')
- new_momentum: float32 [8192, 512], P('fsdp')
The draws below stay inside these ranges and needn't reach their ends.
All inputs are finite; a program needn't handle non-finite values.
Results may differ from the reference program's by a relative error of at most 0.0003.
Values may be sent and summed in bfloat16 or wider, within the bound.
No kernel may reach another device: no remote copies, remote signals or barrier semaphores. Data moves between devices by JAX's collectives and lax.ppermute only.
A program may use at most 128 MiB of HBM per device.

```python
import math
import jax
import jax.numpy as jnp
from jax import lax

D = 8192
VCOLS = 512
TOK_DEV = 192
WORKERS = 2
TOKENS = 6144
N_WORKER = 2
N_FSDP = 16


def spiked(entries, stream_key, source, target, shards_of, factor):
    owner, partner = [(jnp.arange(entries.shape[position]) // (entries.shape[position] // shards_of)).reshape([-1 if axis == position else 1 for axis in range(entries.ndim)]) for position in (source, target)]
    chosen = jax.random.permutation(stream_key, shards_of)[partner]
    strong = (owner == chosen) | (owner == (partner + shards_of // 2) % shards_of)
    return jnp.where(strong, factor * entries, entries)


def shard_levels(rng, shape, split, smallest, largest):
    def one(axis_at, shards_of):
        heights = jax.random.uniform(jax.random.fold_in(jax.random.fold_in(rng, 6), axis_at), (shards_of,), jnp.float32, smallest / len(split), largest / len(split))
        return jnp.repeat(jnp.exp(heights), shape[axis_at] // shards_of).reshape((-1,) + (1,) * (len(shape) - axis_at - 1))

    loudness = one(*split[0])
    for cut in split[1:]:
        loudness = loudness * one(*cut)
    return loudness


def scatter_about(own_key, shape, scale, most, split=(), kind=jnp.bfloat16):
    loudness = shard_levels(own_key, shape, split, -0.22, 0.18) if split else 1.0
    result = jax.random.normal(own_key, shape, jnp.float32) * scale * loudness
    return jnp.minimum(jnp.maximum(result, -most), most).astype(kind)


def gaussian_with(key, shape, deviation, reach, cuts, heavy, kind=jnp.bfloat16):
    values = deviation * jax.random.normal(key, shape, jnp.float32)
    if cuts:
        values = values * shard_levels(key, shape, cuts, -0.22, 0.18)
    return jnp.clip(spiked(values, jax.random.fold_in(key, 3), *heavy), -reach, reach).astype(kind)


def setup_inputs(seed: int = 0) -> dict:
    keys = jax.random.split(jax.random.key(seed), 9)
    features = gaussian_with(keys[0], (TOKENS, D), 1.0, 6.0, ((0, 32),), (0, 1, 32, 2.75))
    value_cotangent = scatter_about(keys[1], (TOKENS, VCOLS), 1.0, 6.0, ((0, 32),))
    value_weight = scatter_about(keys[2], (WORKERS, D, VCOLS), VCOLS ** -0.5, 0.25, ((0, 2), (1, 16)), jnp.float32)
    first_moment = scatter_about(keys[3], (WORKERS, D, VCOLS), 8.0, 48.0, ((0, 2), (1, 16)), jnp.float32)
    second_moment = jnp.clip(jnp.exp(math.log(10000.0) - 2.3025851 * jax.random.uniform(keys[4], (WORKERS, D, VCOLS), jnp.float32) ** shard_levels(keys[4], (WORKERS, D, VCOLS), ((0, 2), (1, 16)), -0.2, 0.2)), 1000.0, 10000.0)
    fragment_local = scatter_about(keys[5], (WORKERS, D, VCOLS), 1.0, 6.0, ((0, 2), (1, 16)), jnp.float32)
    fragment_anchor = scatter_about(keys[6], (D, VCOLS), 1.0, 6.0, ((0, 16),), jnp.float32)
    outer_momentum = scatter_about(keys[7], (D, VCOLS), 0.5, 3.0, ((0, 16),), jnp.float32)
    return dict(features=features, value_cotangent=value_cotangent, value_weight=value_weight, first_moment=first_moment, second_moment=second_moment, fragment_local=fragment_local, fragment_anchor=fragment_anchor, outer_momentum=outer_momentum)


first_decay = 0.9
second_decay = 0.95
inner_rate = 0.001
weight_decay = 0.1
adam_epsilon = 1e-08
adam_count = 10.0
outer_rate = 0.7
outer_mass = 0.9

def reference(features, value_cotangent, value_weight, first_moment, second_moment, fragment_local, fragment_anchor, outer_momentum):
    group_rows = TOK_DEV * N_FSDP
    grads_out = []
    weights_out = []
    firsts_out = []
    seconds_out = []
    for worker_id in range(N_WORKER):
        rows_in = features[worker_id * group_rows:(worker_id + 1) * group_rows]
        rows_cot = value_cotangent[worker_id * group_rows:(worker_id + 1) * group_rows]
        weight = value_weight[worker_id]
        grads_out.append(jnp.dot(rows_cot.astype(jnp.float32), weight.T, preferred_element_type=jnp.float32, precision=lax.Precision.HIGHEST))
        gradient = jnp.dot(rows_in.T, rows_cot, preferred_element_type=jnp.float32)
        first_new = first_decay * first_moment[worker_id] + (1.0 - first_decay) * gradient
        second_new = second_decay * second_moment[worker_id] + (1.0 - second_decay) * gradient * gradient
        first_hat = first_new / (1.0 - first_decay ** adam_count)
        second_hat = second_new / (1.0 - second_decay ** adam_count)
        weights_out.append(weight - inner_rate * (first_hat / (jnp.sqrt(second_hat) + adam_epsilon) + weight_decay * weight))
        firsts_out.append(first_new)
        seconds_out.append(second_new)
    pseudo_mean = lax.optimization_barrier(jnp.sum(fragment_anchor[None] - fragment_local, axis=0)) / N_WORKER
    new_momentum = outer_mass * outer_momentum + pseudo_mean
    new_anchor = fragment_anchor - outer_rate * (pseudo_mean + outer_mass * new_momentum)
    return (jnp.concatenate(grads_out, axis=0), jnp.stack(weights_out), jnp.stack(firsts_out), jnp.stack(seconds_out), new_anchor, new_momentum)
```

```python
import functools

import jax
import jax.numpy as jnp
from jax import lax
from jax.experimental import pallas as pl
from jax.experimental.pallas import tpu as pltpu
from jax.sharding import PartitionSpec as P

first_decay = 0.9
second_decay = 0.95
inner_rate = 0.001
weight_decay = 0.1
adam_epsilon = 1e-08
adam_count = 10.0
outer_rate = 0.7
outer_mass = 0.9

PLANE = 4
WEIGHT_SCALE = 2.0**17
WIRE = jnp.bfloat16


def power_below(limit):
    scale = 1.0
    while scale * limit > 32768.0:
        scale /= 2.0
    while scale * limit < 16384.0:
        scale *= 2.0
    return scale


def encode(x):
    power = x * x
    power = power * power
    power = power * power
    return jnp.where(x < 0.0, -power, power).astype(WIRE)


def decode(code):
    wide = code.astype(jnp.float32)
    size = jnp.abs(wide)
    root = jnp.where(size > 0.0, jnp.exp(jnp.log(size) * 0.125), 0.0)
    return jnp.where(wide < 0.0, -root, root)


def vmem(count):
    return [pl.BlockSpec(memory_space=pltpu.VMEM)] * count


def contract(left, right, dims):
    return lax.dot_general(left, right, (dims, ((), ())), preferred_element_type=jnp.float32)


def pack_kernel(columns, planes, axis, features, weight, coded, *outs_and_sem):
    outs, sem = outs_and_sem[:-1], outs_and_sem[-1]
    me = lax.axis_index(axis)
    z, p = me // PLANE, me % PLANE
    copies = []
    for at in range(planes):
        block = lax.rem(z + 2 * planes - 1 - at, planes)
        for k in range(PLANE):
            start = pl.multiple_of((block * PLANE + (p ^ k)) * columns, 128)
            copy = pltpu.make_async_copy(
                features.at[:, pl.ds(start, columns)], outs[at * PLANE + k], sem.at[at * PLANE + k]
            )
            copy.start()
            copies.append(copy)
    coded[...] = encode(weight[...] * WEIGHT_SCALE)
    for copy in copies:
        copy.wait()


def pack(features, weight, columns, planes):
    rows = features.shape[0]
    count = planes * PLANE
    coded, *outs = pl.pallas_call(
        functools.partial(pack_kernel, columns, planes, "fsdp"),
        out_shape=[jax.ShapeDtypeStruct(weight.shape, WIRE)]
        + [jax.ShapeDtypeStruct((rows, columns), features.dtype)] * count,
        in_specs=[pl.BlockSpec(memory_space=pl.ANY), *vmem(1)],
        out_specs=vmem(1) + [pl.BlockSpec(memory_space=pl.ANY)] * count,
        scratch_shapes=[pltpu.SemaphoreType.DMA((count,))],
        name="pack",
    )(features, weight)
    return coded, [outs[at * PLANE : (at + 1) * PLANE] for at in range(planes)]


def partial_kernel(scale, *refs):
    parts, cots, so_far, out = refs[:PLANE], refs[PLANE : 2 * PLANE], refs[2 * PLANE : -1], refs[-1]
    total = contract(parts[0][...], cots[0][...], ((0,), (0,)))
    for part, cot in zip(parts[1:], cots[1:]):
        total += contract(part[...], cot[...], ((0,), (0,)))
    total = total * scale
    for ref in so_far:
        total += decode(ref[...])
    out[...] = encode(total) if out.dtype == WIRE else total


def plane_partial(parts, cots, so_far, scale, dtype):
    shape = (parts[0].shape[1], cots[0].shape[1])
    operands = [*parts, *cots, *so_far]
    return pl.pallas_call(
        functools.partial(partial_kernel, scale),
        out_shape=jax.ShapeDtypeStruct(shape, dtype),
        in_specs=vmem(len(operands)),
        out_specs=pl.BlockSpec(memory_space=pltpu.VMEM),
        compiler_params=pltpu.CompilerParams(vmem_limit_bytes=24 << 20),
        name="plane_partial",
    )(*operands)


def product_kernel(factor, scale, *refs):
    weight, cots, outs = refs[0], refs[1 : 1 + PLANE], refs[1 + PLANE :]
    wide = decode(weight[...]) if weight.dtype == WIRE else weight[...]
    high = wide.astype(jnp.bfloat16)
    low = (wide - high.astype(jnp.float32)).astype(jnp.bfloat16)
    for k in range(PLANE):
        cot = cots[k][...]
        result = contract(cot, high, ((1,), (1,))) + contract(cot, low, ((1,), (1,)))
        outs[k][...] = result * factor if k == 0 else encode(result * (factor * scale))


def plane_product(weight, cots, factor, scale):
    shape = (cots[0].shape[0], weight.shape[0])
    return pl.pallas_call(
        functools.partial(product_kernel, factor, scale),
        out_shape=[jax.ShapeDtypeStruct(shape, jnp.float32 if k == 0 else WIRE) for k in range(PLANE)],
        in_specs=vmem(1 + PLANE),
        out_specs=vmem(PLANE),
        compiler_params=pltpu.CompilerParams(vmem_limit_bytes=24 << 20),
        name="plane_product",
    )(weight, *cots)


def unpack_kernel(columns, planes, axis, factor, *refs):
    count = planes * PLANE
    pieces, out, buffer, sem = refs[:count], refs[count], refs[count + 1], refs[count + 2]
    me = lax.axis_index(axis)
    z, p = me // PLANE, me % PLANE
    copies = []
    for at in range(planes):
        block = lax.rem(z + planes - at, planes)
        for k in range(PLANE):
            i = at * PLANE + k
            if k == 0:
                source = pieces[i]
            else:
                buffer[i] = decode(pieces[i][...]) * factor
                source = buffer.at[i]
            start = pl.multiple_of((block * PLANE + (p ^ k)) * columns, 128)
            copy = pltpu.make_async_copy(source, out.at[:, pl.ds(start, columns)], sem.at[i])
            copy.start()
            copies.append(copy)
    for copy in copies:
        copy.wait()


def unpack(pieces, planes, factor):
    rows, columns = pieces[0].shape
    count = planes * PLANE
    return pl.pallas_call(
        functools.partial(unpack_kernel, columns, planes, "fsdp", factor),
        out_shape=jax.ShapeDtypeStruct((rows, columns * count), jnp.float32),
        in_specs=vmem(count),
        out_specs=pl.BlockSpec(memory_space=pl.ANY),
        scratch_shapes=[
            pltpu.VMEM((count, rows, columns), jnp.float32),
            pltpu.SemaphoreType.DMA((count,)),
        ],
        compiler_params=pltpu.CompilerParams(vmem_limit_bytes=40 << 20),
        name="unpack",
    )(*pieces)


def on_device(
    features,
    value_cotangent,
    value_weight,
    first_moment,
    second_moment,
    fragment_local,
    fragment_anchor,
    outer_momentum,
):
    size = lax.axis_size("fsdp")
    planes = size // PLANE
    columns = features.shape[1] // size
    tokens = features.shape[0] * size
    gradient_scale = power_below(tokens * 24.0 * 6.0)
    product_scale = power_below(value_cotangent.shape[1] * 6.0 * 0.25)

    ring = [(i, (i + PLANE) % size) for i in range(size)]

    def around(x):
        return lax.ppermute(x, "fsdp", ring)

    def across(x, k):
        return lax.ppermute(x, "fsdp", [(i, i ^ k) for i in range(size)])

    weight = value_weight[0]
    cots = [value_cotangent] + [across(value_cotangent, k) for k in range(1, PLANE)]
    travelling, packed = pack(features, weight, columns, planes)
    weights = [weight]
    for _ in range(1, planes):
        travelling = around(travelling)
        weights.append(travelling)

    received = [[part if k == 0 else across(part, k) for k, part in enumerate(parts)] for parts in packed]

    pieces = []
    for held in weights:
        products = plane_product(held, cots, 1.0 if held is weight else 1.0 / WEIGHT_SCALE, product_scale)
        pieces += [part if k == 0 else across(part, k) for k, part in enumerate(products)]
    feature_grad = unpack(pieces, planes, 1.0 / product_scale)

    running = []
    for at, parts in enumerate(received):
        last = at == planes - 1
        total = plane_partial(parts, cots, running, gradient_scale, jnp.float32 if last else WIRE)
        running = [total if last else around(total)]
    gradient = running[0] * (1.0 / gradient_scale)

    first_new = first_decay * first_moment[0] + (1.0 - first_decay) * gradient
    second_new = second_decay * second_moment[0] + (1.0 - second_decay) * gradient * gradient
    first_hat = first_new / (1.0 - first_decay**adam_count)
    second_hat = second_new / (1.0 - second_decay**adam_count)
    weight_new = weight - inner_rate * (
        first_hat / (jnp.sqrt(second_hat) + adam_epsilon) + weight_decay * weight
    )
    workers = lax.axis_size("worker")
    difference = fragment_anchor - fragment_local[0]
    if workers == 2:
        pseudo_sum = difference + lax.ppermute(difference, "worker", [(0, 1), (1, 0)])
    else:
        pseudo_sum = lax.psum(difference, "worker")
    pseudo_mean = pseudo_sum / workers
    new_momentum = outer_mass * outer_momentum + pseudo_mean
    new_anchor = fragment_anchor - outer_rate * (pseudo_mean + outer_mass * new_momentum)
    return (
        feature_grad,
        weight_new[None],
        first_new[None],
        second_new[None],
        new_anchor,
        new_momentum,
    )


def solution(mesh):
    placed = (
        P(("worker", "fsdp"), None),
        P(("worker", "fsdp"), None),
        P("worker", "fsdp", None),
        P("worker", "fsdp", None),
        P("worker", "fsdp", None),
        P("worker", "fsdp", None),
        P("fsdp", None),
        P("fsdp", None),
    )
    return jax.shard_map(
        on_device,
        mesh=mesh,
        in_specs=placed,
        out_specs=(
            P(("worker", "fsdp"), None),
            P("worker", "fsdp", None),
            P("worker", "fsdp", None),
            P("worker", "fsdp", None),
            P("fsdp", None),
            P("fsdp", None),
        ),
        check_vma=False,
    )
```

```python
import functools

import jax
import jax.numpy as jnp
from jax import lax
from jax.experimental import pallas as pl
from jax.experimental.pallas import tpu as pltpu
from jax.sharding import PartitionSpec as P

first_decay = 0.9
second_decay = 0.95
inner_rate = 0.001
weight_decay = 0.1
adam_epsilon = 1e-08
adam_count = 10.0
outer_rate = 0.7
outer_mass = 0.9

PLANE = 4
WEIGHT_SCALE = 2.0**17
WIRE = jnp.bfloat16


def power_below(limit):
    scale = 1.0
    while scale * limit > 32768.0:
        scale /= 2.0
    while scale * limit < 16384.0:
        scale *= 2.0
    return scale


def encode(x):
    power = x * x
    power = power * power
    power = power * power
    return jnp.where(x < 0.0, -power, power).astype(WIRE)


def decode(code):
    wide = code.astype(jnp.float32)
    size = jnp.abs(wide)
    root = jnp.where(size > 0.0, jnp.exp(jnp.log(size) * 0.125), 0.0)
    return jnp.where(wide < 0.0, -root, root)


def vmem(count):
    return [pl.BlockSpec(memory_space=pltpu.VMEM)] * count


def contract(left, right, dims):
    return lax.dot_general(left, right, (dims, ((), ())), preferred_element_type=jnp.float32)


def pack_kernel(columns, planes, axis, features, cot, weight, coded, own, *chunks):
    me = lax.axis_index(axis)
    z, p = me // PLANE, me % PLANE
    coded[...] = encode(weight[...] * WEIGHT_SCALE)
    for k in range(PLANE):
        if k > 0:
            first, rest = chunks[2 * k - 2], chunks[2 * k - 1]
            first[:, : cot.shape[1]] = cot[...]
        for at in range(planes):
            block = lax.rem(z + 2 * planes - 1 - at, planes)
            start = pl.multiple_of((block * PLANE + (p ^ k)) * columns, 128)
            value = features[:, pl.ds(start, columns)]
            if k == 0:
                own[:, at * columns : (at + 1) * columns] = value
            elif at == 0:
                first[:, cot.shape[1] :] = value
            else:
                rest[:, (at - 1) * columns : at * columns] = value


def pack(features, cot, weight, columns, planes):
    rows = features.shape[0]
    widths = [planes * columns] + [cot.shape[1] + columns, (planes - 1) * columns] * (PLANE - 1)
    coded, own, *chunks = pl.pallas_call(
        functools.partial(pack_kernel, columns, planes, "fsdp"),
        out_shape=[jax.ShapeDtypeStruct(weight.shape, WIRE)]
        + [jax.ShapeDtypeStruct((rows, width), features.dtype) for width in widths],
        in_specs=vmem(3),
        out_specs=vmem(1 + len(widths)),
        compiler_params=pltpu.CompilerParams(vmem_limit_bytes=32 << 20),
        name="pack",
    )(features, cot, weight)
    return coded, own, [chunks[2 * k : 2 * k + 2] for k in range(PLANE - 1)]


def partial_kernel(at, columns, scale, own, cot, *refs):
    firsts, others, so_far, out = refs[:3], refs[3:-1], (), refs[-1]
    if at > 0:
        others, so_far = refs[3:6], refs[6:-1]
    depth = cot.shape[1]
    total = contract(own[:, at * columns : (at + 1) * columns], cot[...], ((0,), (0,)))
    for i, first in enumerate(firsts):
        if at == 0:
            part = first[:, depth:]
        else:
            part = others[i][:, (at - 1) * columns : at * columns]
        total += contract(part, first[:, :depth], ((0,), (0,)))
    total = total * scale
    for ref in so_far:
        total += decode(ref[...])
    out[...] = encode(total) if out.dtype == WIRE else total


def plane_partial(at, own, cot, firsts, others, so_far, columns, scale, dtype):
    operands = [own, cot, *firsts, *others, *so_far]
    return pl.pallas_call(
        functools.partial(partial_kernel, at, columns, scale),
        out_shape=jax.ShapeDtypeStruct((columns, cot.shape[1]), dtype),
        in_specs=vmem(len(operands)),
        out_specs=pl.BlockSpec(memory_space=pltpu.VMEM),
        compiler_params=pltpu.CompilerParams(vmem_limit_bytes=32 << 20),
        name="plane_partial",
    )(*operands)


def product_kernel(count, scale, *refs):
    weights, cot, firsts, outs = refs[:count], refs[count], refs[count + 1 : count + PLANE], refs[count + PLANE :]
    depth = cot.shape[1]
    for i, weight in enumerate(weights):
        if weight.dtype == WIRE:
            wide, factor = decode(weight[...]), 1.0 / WEIGHT_SCALE
        else:
            wide, factor = weight[...], 1.0
        high = wide.astype(jnp.bfloat16)
        low = (wide - high.astype(jnp.float32)).astype(jnp.bfloat16)
        columns = weight.shape[0]
        for k in range(PLANE):
            rows = cot[...] if k == 0 else firsts[k - 1][:, :depth]
            result = contract(rows, high, ((1,), (1,))) + contract(rows, low, ((1,), (1,)))
            result = result * factor if k == 0 else encode(result * (factor * scale))
            outs[k][:, i * columns : (i + 1) * columns] = result


def plane_product(weights, cot, firsts, scale):
    shape = (cot.shape[0], weights[0].shape[0] * len(weights))
    return pl.pallas_call(
        functools.partial(product_kernel, len(weights), scale),
        out_shape=[jax.ShapeDtypeStruct(shape, jnp.float32 if k == 0 else WIRE) for k in range(PLANE)],
        in_specs=vmem(len(weights) + PLANE),
        out_specs=vmem(PLANE),
        compiler_params=pltpu.CompilerParams(vmem_limit_bytes=32 << 20),
        name="plane_product",
    )(*weights, cot, *firsts)


def unpack_kernel(columns, planes, axis, factor, widths, *refs):
    pieces, out, buffer, sem = refs[:-3], refs[-3], refs[-2], refs[-1]
    me = lax.axis_index(axis)
    z, p = me // PLANE, me % PLANE
    copies = []
    at = 0
    for chunk, width in enumerate(widths):
        for inner in range(width):
            block = lax.rem(z + planes - at, planes)
            for k in range(PLANE):
                i = at * PLANE + k
                piece = pieces[chunk * PLANE + k]
                span = slice(inner * columns, (inner + 1) * columns)
                if k == 0:
                    source = piece.at[:, span]
                else:
                    buffer[i] = decode(piece[:, span]) * factor
                    source = buffer.at[i]
                start = pl.multiple_of((block * PLANE + (p ^ k)) * columns, 128)
                copy = pltpu.make_async_copy(source, out.at[:, pl.ds(start, columns)], sem.at[i])
                copy.start()
                copies.append(copy)
            at += 1
    for copy in copies:
        copy.wait()


def unpack(pieces, columns, planes, factor):
    rows = pieces[0].shape[0]
    count = planes * PLANE
    widths = [piece.shape[1] // columns for piece in pieces[::PLANE]]
    return pl.pallas_call(
        functools.partial(unpack_kernel, columns, planes, "fsdp", factor, widths),
        out_shape=jax.ShapeDtypeStruct((rows, columns * count), jnp.float32),
        in_specs=vmem(len(pieces)),
        out_specs=pl.BlockSpec(memory_space=pl.ANY),
        scratch_shapes=[
            pltpu.VMEM((count, rows, columns), jnp.float32),
            pltpu.SemaphoreType.DMA((count,)),
        ],
        compiler_params=pltpu.CompilerParams(vmem_limit_bytes=40 << 20),
        name="unpack",
    )(*pieces)


def on_device(
    features,
    value_cotangent,
    value_weight,
    first_moment,
    second_moment,
    fragment_local,
    fragment_anchor,
    outer_momentum,
):
    size = lax.axis_size("fsdp")
    planes = size // PLANE
    columns = features.shape[1] // size
    tokens = features.shape[0] * size
    gradient_scale = power_below(tokens * 24.0 * 6.0)
    product_scale = power_below(value_cotangent.shape[1] * 6.0 * 0.25)

    ring = [(i, (i + PLANE) % size) for i in range(size)]

    def around(x):
        return lax.ppermute(x, "fsdp", ring)

    def across(x, k):
        return lax.ppermute(x, "fsdp", [(i, i ^ k) for i in range(size)])

    weight = value_weight[0]
    travelling, own, chunks = pack(features, value_cotangent, weight, columns, planes)
    weights = [weight]
    for _ in range(1, planes):
        travelling = around(travelling)
        weights.append(travelling)
    firsts = [across(first, k + 1) for k, (first, _) in enumerate(chunks)]
    others = [across(rest, k + 1) for k, (_, rest) in enumerate(chunks)]

    pieces = []
    for half in (weights[: planes // 2], weights[planes // 2 :]):
        products = plane_product(half, value_cotangent, firsts, product_scale)
        pieces += [part if k == 0 else across(part, k) for k, part in enumerate(products)]
    feature_grad = unpack(pieces, columns, planes, 1.0 / product_scale)

    running = []
    for at in range(planes):
        last = at == planes - 1
        total = plane_partial(
            at,
            own,
            value_cotangent,
            firsts,
            others if at > 0 else [],
            running,
            columns,
            gradient_scale,
            jnp.float32 if last else WIRE,
        )
        running = [total if last else around(total)]
    gradient = running[0] * (1.0 / gradient_scale)

    first_new = first_decay * first_moment[0] + (1.0 - first_decay) * gradient
    second_new = second_decay * second_moment[0] + (1.0 - second_decay) * gradient * gradient
    first_hat = first_new / (1.0 - first_decay**adam_count)
    second_hat = second_new / (1.0 - second_decay**adam_count)
    weight_new = weight - inner_rate * (
        first_hat / (jnp.sqrt(second_hat) + adam_epsilon) + weight_decay * weight
    )
    workers = lax.axis_size("worker")
    difference = fragment_anchor - fragment_local[0]
    if workers == 2:
        pseudo_sum = difference + lax.ppermute(difference, "worker", [(0, 1), (1, 0)])
    else:
        pseudo_sum = lax.psum(difference, "worker")
    pseudo_mean = pseudo_sum / workers
    new_momentum = outer_mass * outer_momentum + pseudo_mean
    new_anchor = fragment_anchor - outer_rate * (pseudo_mean + outer_mass * new_momentum)
    return (
        feature_grad,
        weight_new[None],
        first_new[None],
        second_new[None],
        new_anchor,
        new_momentum,
    )


def solution(mesh):
    placed = (
        P(("worker", "fsdp"), None),
        P(("worker", "fsdp"), None),
        P("worker", "fsdp", None),
        P("worker", "fsdp", None),
        P("worker", "fsdp", None),
        P("worker", "fsdp", None),
        P("fsdp", None),
        P("fsdp", None),
    )
    return jax.shard_map(
        on_device,
        mesh=mesh,
        in_specs=placed,
        out_specs=(
            P(("worker", "fsdp"), None),
            P("worker", "fsdp", None),
            P("worker", "fsdp", None),
            P("worker", "fsdp", None),
            P("fsdp", None),
            P("fsdp", None),
        ),
        check_vma=False,
    )
```

```python
import functools

import jax
import jax.numpy as jnp
from jax import lax
from jax.experimental import pallas as pl
from jax.experimental.pallas import tpu as pltpu
from jax.sharding import PartitionSpec as P

first_decay = 0.9
second_decay = 0.95
inner_rate = 0.001
weight_decay = 0.1
adam_epsilon = 1e-08
adam_count = 10.0
outer_rate = 0.7
outer_mass = 0.9

PLANE = 4
WEIGHT_SCALE = 2.0**17
WIRE = jnp.bfloat16
SPAN = pl.CostEstimate(flops=1 << 36, bytes_accessed=1 << 30, transcendentals=0)


def power_below(limit):
    scale = 1.0
    while scale * limit > 32768.0:
        scale /= 2.0
    while scale * limit < 16384.0:
        scale *= 2.0
    return scale


def encode(x):
    power = x * x
    power = power * power
    power = power * power
    return jnp.where(x < 0.0, -power, power).astype(WIRE)


def decode(code):
    wide = code.astype(jnp.float32)
    size = jnp.abs(wide)
    root = jnp.where(size > 0.0, jnp.exp(jnp.log(size) * 0.125), 0.0)
    return jnp.where(wide < 0.0, -root, root)


def vmem(count):
    return [pl.BlockSpec(memory_space=pltpu.VMEM)] * count


def contract(left, right, dims):
    return lax.dot_general(left, right, (dims, ((), ())), preferred_element_type=jnp.float32)


def pack_kernel(columns, planes, axis, features_far, cot_in, weight_far, coded, weight, cot, own, *refs):
    chunks, (features, sem) = refs[:-2], refs[-2:]
    me = lax.axis_index(axis)
    z, p = me // PLANE, me % PLANE
    copies = [
        pltpu.make_async_copy(weight_far.at[0], weight, sem.at[0]),
        pltpu.make_async_copy(features_far, features, sem.at[1]),
    ]
    for copy in copies:
        copy.start()
    cot[...] = cot_in[...]
    copies[0].wait()
    coded[...] = encode(weight[...] * WEIGHT_SCALE)
    copies[1].wait()
    for k in range(PLANE):
        if k > 0:
            first, rest = chunks[2 * k - 2], chunks[2 * k - 1]
            first[:, : cot.shape[1]] = cot[...]
        for at in range(planes):
            block = lax.rem(z + 2 * planes - 1 - at, planes)
            start = pl.multiple_of((block * PLANE + (p ^ k)) * columns, 128)
            value = features[:, pl.ds(start, columns)]
            if k == 0:
                own[:, at * columns : (at + 1) * columns] = value
            elif at == 0:
                first[:, cot.shape[1] :] = value
            else:
                rest[:, (at - 1) * columns : at * columns] = value


def pack(features, cot, weight, columns, planes):
    rows = features.shape[0]
    widths = [planes * columns] + [cot.shape[1] + columns, (planes - 1) * columns] * (PLANE - 1)
    coded, weight, cot, own, *chunks = pl.pallas_call(
        functools.partial(pack_kernel, columns, planes, "fsdp"),
        out_shape=[
            jax.ShapeDtypeStruct(weight.shape[1:], WIRE),
            jax.ShapeDtypeStruct(weight.shape[1:], weight.dtype),
            jax.ShapeDtypeStruct(cot.shape, cot.dtype),
        ]
        + [jax.ShapeDtypeStruct((rows, width), features.dtype) for width in widths],
        in_specs=[pl.BlockSpec(memory_space=pltpu.HBM), *vmem(1), pl.BlockSpec(memory_space=pltpu.HBM)],
        out_specs=vmem(3 + len(widths)),
        scratch_shapes=[pltpu.VMEM(features.shape, features.dtype), pltpu.SemaphoreType.DMA((2,))],
        cost_estimate=SPAN,
        compiler_params=pltpu.CompilerParams(vmem_limit_bytes=48 << 20),
        name="pack",
    )(features, cot, weight)
    return coded, weight, cot, own, [chunks[2 * k : 2 * k + 2] for k in range(PLANE - 1)]


def partial_kernel(at, columns, scale, own, cot, *refs):
    firsts, others, so_far, out = refs[:3], refs[3:-1], (), refs[-1]
    if at > 0:
        others, so_far = refs[3:6], refs[6:-1]
    depth = cot.shape[1]
    total = contract(own[:, at * columns : (at + 1) * columns], cot[...], ((0,), (0,)))
    for i, first in enumerate(firsts):
        if at == 0:
            part = first[:, depth:]
        else:
            part = others[i][:, (at - 1) * columns : at * columns]
        total += contract(part, first[:, :depth], ((0,), (0,)))
    total = total * scale
    for ref in so_far:
        total += decode(ref[...])
    out[...] = encode(total) if out.dtype == WIRE else total


def plane_partial(at, own, cot, firsts, others, so_far, columns, scale, dtype):
    operands = [own, cot, *firsts, *others, *so_far]
    return pl.pallas_call(
        functools.partial(partial_kernel, at, columns, scale),
        out_shape=jax.ShapeDtypeStruct((columns, cot.shape[1]), dtype),
        in_specs=vmem(len(operands)),
        out_specs=pl.BlockSpec(memory_space=pltpu.VMEM),
        cost_estimate=SPAN,
        compiler_params=pltpu.CompilerParams(vmem_limit_bytes=32 << 20),
        name="plane_partial",
    )(*operands)


def product_kernel(count, scale, *refs):
    weights, cot, firsts, outs = refs[:count], refs[count], refs[count + 1 : count + PLANE], refs[-PLANE:]
    depth = cot.shape[1]
    for i, weight in enumerate(weights):
        if weight.dtype == WIRE:
            wide, factor = decode(weight[...]), 1.0 / WEIGHT_SCALE
        else:
            wide, factor = weight[...], 1.0
        high = wide.astype(jnp.bfloat16)
        low = (wide - high.astype(jnp.float32)).astype(jnp.bfloat16)
        columns = weight.shape[0]
        for k in range(PLANE):
            rows = cot[...] if k == 0 else firsts[k - 1][:, :depth]
            result = contract(rows, high, ((1,), (1,))) + contract(rows, low, ((1,), (1,)))
            result = result * factor if k == 0 else encode(result * (factor * scale))
            outs[k][:, i * columns : (i + 1) * columns] = result


def product_shapes(weights, cot):
    shape = (cot.shape[0], weights[0].shape[0] * len(weights))
    return [jax.ShapeDtypeStruct(shape, jnp.float32 if k == 0 else WIRE) for k in range(PLANE)]


def plane_product(weights, cot, firsts, after, scale):
    return pl.pallas_call(
        functools.partial(product_kernel, len(weights), scale),
        out_shape=product_shapes(weights, cot),
        in_specs=vmem(len(weights) + PLANE) + [pl.BlockSpec(memory_space=pl.ANY)],
        out_specs=vmem(PLANE),
        cost_estimate=SPAN,
        compiler_params=pltpu.CompilerParams(vmem_limit_bytes=32 << 20),
        name="plane_product",
    )(*weights, cot, *firsts, after)


def unpack_kernel(columns, planes, axis, factor, offsets, *refs):
    pieces, out, buffer, sem = refs[:PLANE], refs[-3], refs[-2], refs[-1]
    me = lax.axis_index(axis)
    z, p = me // PLANE, me % PLANE
    copies = []
    for inner, offset in enumerate(offsets):
        block = lax.rem(z + planes - offset, planes)
        for k in range(PLANE):
            i = inner * PLANE + k
            span = slice(inner * columns, (inner + 1) * columns)
            if k == 0:
                source = pieces[k].at[:, span]
            else:
                buffer[i] = decode(pieces[k][:, span]) * factor
                source = buffer.at[i]
            start = pl.multiple_of((block * PLANE + (p ^ k)) * columns, 128)
            copy = pltpu.make_async_copy(source, out.at[:, pl.ds(start, columns)], sem.at[i])
            copy.start()
            copies.append(copy)
    for copy in copies:
        copy.wait()


def unpack(pieces, out, after, offsets, columns, planes, factor):
    rows = pieces[0].shape[0]
    count = len(offsets) * PLANE
    others = [*out, *after]
    return pl.pallas_call(
        functools.partial(unpack_kernel, columns, planes, "fsdp", factor, offsets),
        out_shape=jax.ShapeDtypeStruct((rows, columns * planes * PLANE), jnp.float32),
        in_specs=vmem(PLANE) + [pl.BlockSpec(memory_space=pl.ANY)] * len(others),
        out_specs=pl.BlockSpec(memory_space=pl.ANY),
        scratch_shapes=[
            pltpu.VMEM((count, rows, columns), jnp.float32),
            pltpu.SemaphoreType.DMA((count,)),
        ],
        input_output_aliases={PLANE: 0} if out else {},
        cost_estimate=SPAN,
        compiler_params=pltpu.CompilerParams(vmem_limit_bytes=32 << 20),
        name="unpack",
    )(*pieces, *others)


def on_device(
    features,
    value_cotangent,
    value_weight,
    first_moment,
    second_moment,
    fragment_local,
    fragment_anchor,
    outer_momentum,
):
    size = lax.axis_size("fsdp")
    planes = size // PLANE
    columns = features.shape[1] // size
    tokens = features.shape[0] * size
    gradient_scale = power_below(tokens * 24.0 * 6.0)
    product_scale = power_below(value_cotangent.shape[1] * 6.0 * 0.25)

    ring = [(i, (i + PLANE) % size) for i in range(size)]

    def around(x):
        return lax.ppermute(x, "fsdp", ring)

    def back(x):
        return lax.ppermute(x, "fsdp", [(to, source) for source, to in ring])

    def across(x, k):
        return lax.ppermute(x, "fsdp", [(i, i ^ k) for i in range(size)])

    workers = lax.axis_size("worker")
    coded, weight, cot, own, chunks = pack(features, value_cotangent, value_weight, columns, planes)
    firsts = [across(first, k + 1) for k, (first, _) in enumerate(chunks)]
    others = [across(rest, k + 1) for k, (_, rest) in enumerate(chunks)]

    early_offsets, late_offsets = (0, 1, planes - 1), tuple(range(2, planes - 1))
    travelling, ahead = around(coded), back(coded)
    travelling, firsts = lax.optimization_barrier((travelling, firsts))
    early_weights, late_weights = [weight, travelling, ahead], []
    for _ in late_offsets:
        travelling = around(travelling)
        late_weights.append(travelling)

    total = plane_partial(0, own, cot, firsts, [], [], columns, gradient_scale, WIRE)
    products = plane_product(early_weights, cot, firsts, total, product_scale)
    early = [part if k == 0 else across(part, k) for k, part in enumerate(products)]
    for at in range(1, planes):
        running = around(total)
        if at == 1:
            running, early[0] = lax.optimization_barrier((running, early[0]))
        last = at == planes - 1
        dtype = jnp.float32 if last else WIRE
        total = plane_partial(at, own, cot, firsts, others, [running], columns, gradient_scale, dtype)
        if at == planes - 2:
            total, fragment_local = lax.optimization_barrier((total, fragment_local))
            mark = total
            products = plane_product(late_weights, cot, firsts, mark, product_scale)
            late = [part if k == 0 else across(part, k) for k, part in enumerate(products)]
    gradient = total * (1.0 / gradient_scale)

    first_new = first_decay * first_moment[0] + (1.0 - first_decay) * gradient
    second_new = second_decay * second_moment[0] + (1.0 - second_decay) * gradient * gradient
    first_hat = first_new / (1.0 - first_decay**adam_count)
    second_hat = second_new / (1.0 - second_decay**adam_count)
    weight_new = weight - inner_rate * (
        first_hat / (jnp.sqrt(second_hat) + adam_epsilon) + weight_decay * weight
    )
    difference = fragment_anchor - fragment_local[0]
    if workers == 2:
        partner_local = lax.ppermute(fragment_local, "worker", [(0, 1), (1, 0)])
        pseudo_sum = difference + (fragment_anchor - partner_local[0])
    else:
        pseudo_sum = lax.psum(difference, "worker")
    pseudo_mean = pseudo_sum / workers
    new_momentum = outer_mass * outer_momentum + pseudo_mean
    new_anchor = fragment_anchor - outer_rate * (pseudo_mean + outer_mass * new_momentum)

    factor = 1.0 / product_scale
    feature_grad = unpack(early, [], [mark], early_offsets, columns, planes, factor)
    feature_grad = unpack(
        late, [feature_grad], [first_new, new_momentum], late_offsets, columns, planes, factor
    )
    return (
        feature_grad,
        weight_new[None],
        first_new[None],
        second_new[None],
        new_anchor,
        new_momentum,
    )


def solution(mesh):
    placed = (
        P(("worker", "fsdp"), None),
        P(("worker", "fsdp"), None),
        P("worker", "fsdp", None),
        P("worker", "fsdp", None),
        P("worker", "fsdp", None),
        P("worker", "fsdp", None),
        P("fsdp", None),
        P("fsdp", None),
    )
    return jax.shard_map(
        on_device,
        mesh=mesh,
        in_specs=placed,
        out_specs=(
            P(("worker", "fsdp"), None),
            P("worker", "fsdp", None),
            P("worker", "fsdp", None),
            P("worker", "fsdp", None),
            P("fsdp", None),
            P("fsdp", None),
        ),
        check_vma=False,
    )
```

```python
import functools

import jax
import jax.numpy as jnp
from jax import lax
from jax.experimental import pallas as pl
from jax.experimental.pallas import tpu as pltpu
from jax.sharding import PartitionSpec as P

first_decay = 0.9
second_decay = 0.95
inner_rate = 0.001
weight_decay = 0.1
adam_epsilon = 1e-08
adam_count = 10.0
outer_rate = 0.7
outer_mass = 0.9

PLANE = 4
WEIGHT_SCALE = 2.0**17
WIRE = jnp.bfloat16
C_PARTIAL, C_PRODUCT, C_UNPACK = (33, 36, 34), (33, 20), (32, 30)


def cost(log_flops):
    return pl.CostEstimate(flops=1 << log_flops, bytes_accessed=1 << 20, transcendentals=0)


def power_below(limit):
    scale = 1.0
    while scale * limit > 32768.0:
        scale /= 2.0
    while scale * limit < 16384.0:
        scale *= 2.0
    return scale


def encode(x):
    power = x * x
    power = power * power
    power = power * power
    return jnp.where(x < 0.0, -power, power).astype(WIRE)


def decode(code):
    wide = code.astype(jnp.float32)
    size = jnp.abs(wide)
    root = jnp.where(size > 0.0, jnp.exp(jnp.log(size) * 0.125), 0.0)
    return jnp.where(wide < 0.0, -root, root)


def vmem(count):
    return [pl.BlockSpec(memory_space=pltpu.VMEM)] * count


def contract(left, right, dims):
    return lax.dot_general(left, right, (dims, ((), ())), preferred_element_type=jnp.float32)


def pack_kernel(columns, distances, axis, features_far, cot_in, weight_far, coded, weight, cot, own, *refs):
    chunks, (features, sem) = refs[:-2], refs[-2:]
    me = lax.axis_index(axis)
    z, p, planes = me // PLANE, me % PLANE, len(distances)
    copies = [
        pltpu.make_async_copy(weight_far.at[0], weight, sem.at[0]),
        pltpu.make_async_copy(features_far, features, sem.at[1]),
    ]
    for copy in copies:
        copy.start()
    cot[...] = cot_in[...]
    copies[0].wait()
    coded[...] = encode(weight[...] * WEIGHT_SCALE)
    copies[1].wait()
    for k in range(PLANE):
        if k > 0:
            first, rest = chunks[2 * k - 2], chunks[2 * k - 1]
            first[:, : cot.shape[1]] = cot[...]
        for at, distance in enumerate(distances):
            block = lax.rem(z + planes + distance, planes)
            start = pl.multiple_of((block * PLANE + (p ^ k)) * columns, 128)
            value = features[:, pl.ds(start, columns)]
            if k == 0:
                own[:, at * columns : (at + 1) * columns] = value
            elif at == 0:
                first[:, cot.shape[1] :] = value
            else:
                rest[:, (at - 1) * columns : at * columns] = value


def pack(features, cot, weight, columns, distances):
    rows, planes = features.shape[0], len(distances)
    widths = [planes * columns] + [cot.shape[1] + columns, (planes - 1) * columns] * (PLANE - 1)
    coded, weight, cot, own, *chunks = pl.pallas_call(
        functools.partial(pack_kernel, columns, distances, "fsdp"),
        out_shape=[
            jax.ShapeDtypeStruct(weight.shape[1:], WIRE),
            jax.ShapeDtypeStruct(weight.shape[1:], weight.dtype),
            jax.ShapeDtypeStruct(cot.shape, cot.dtype),
        ]
        + [jax.ShapeDtypeStruct((rows, width), features.dtype) for width in widths],
        in_specs=[pl.BlockSpec(memory_space=pltpu.HBM), *vmem(1), pl.BlockSpec(memory_space=pltpu.HBM)],
        out_specs=vmem(3 + len(widths)),
        scratch_shapes=[pltpu.VMEM(features.shape, features.dtype), pltpu.SemaphoreType.DMA((2,))],
        cost_estimate=cost(36),
        compiler_params=pltpu.CompilerParams(vmem_limit_bytes=48 << 20),
        name="pack",
    )(features, cot, weight)
    return coded, weight, cot, own, [chunks[2 * k : 2 * k + 2] for k in range(PLANE - 1)]


def partial_kernel(columns, scale, spread, own, cot, *refs):
    firsts, refs = refs[: PLANE - 1], refs[PLANE - 1 :]
    others = refs[: PLANE - 1] if any(at > 0 for at, _, _ in spread) else ()
    rest, outs = refs[len(others) : -len(spread)], refs[-len(spread) :]
    depth = cot.shape[1]
    for (at, count, rides), out in zip(spread, outs):
        total = contract(own[:, at * columns : (at + 1) * columns], cot[...], ((0,), (0,)))
        for i, first in enumerate(firsts):
            if at == 0:
                part = first[:, depth:]
            else:
                part = others[i][:, (at - 1) * columns : at * columns]
            total += contract(part, first[:, :depth], ((0,), (0,)))
        total = total * scale
        for ref in rest[:count]:
            total += decode(ref[:columns, :])
        out[:columns, :] = encode(total) if out.dtype == WIRE else total
        if rides:
            out[columns:, :] = rest[count][-columns:, :]
        rest = rest[count + rides :]


def plane_partial(spread, own, cot, firsts, others, rest, columns, scale, dtype, span):
    operands = [own, cot, *firsts, *others, *rest]
    outs = pl.pallas_call(
        functools.partial(partial_kernel, columns, scale, spread),
        out_shape=[jax.ShapeDtypeStruct((columns * (1 + rides), cot.shape[1]), dtype) for _, _, rides in spread],
        in_specs=vmem(len(operands)),
        out_specs=vmem(len(spread)),
        cost_estimate=cost(span),
        compiler_params=pltpu.CompilerParams(vmem_limit_bytes=32 << 20),
        name="plane_partial",
    )(*operands)
    return list(outs)


def product_kernel(columns, count, scale, *refs):
    weights, cot, firsts, outs = refs[:count], refs[count], refs[count + 1 : count + PLANE], refs[-PLANE:]
    depth = cot.shape[1]
    for i, weight in enumerate(weights):
        if weight.dtype == WIRE:
            wide, factor = decode(weight[-columns:, :]), 1.0 / WEIGHT_SCALE
        else:
            wide, factor = weight[...], 1.0
        high = wide.astype(jnp.bfloat16)
        low = (wide - high.astype(jnp.float32)).astype(jnp.bfloat16)
        for k in range(PLANE):
            rows = cot[...] if k == 0 else firsts[k - 1][:, :depth]
            result = contract(rows, high, ((1,), (1,))) + contract(rows, low, ((1,), (1,)))
            result = result * factor if k == 0 else encode(result * (factor * scale))
            outs[k][:, i * columns : (i + 1) * columns] = result


def plane_product(weights, cot, firsts, after, columns, scale, span):
    shape = (cot.shape[0], columns * len(weights))
    outs = pl.pallas_call(
        functools.partial(product_kernel, columns, len(weights), scale),
        out_shape=[jax.ShapeDtypeStruct(shape, jnp.float32 if k == 0 else WIRE) for k in range(PLANE)],
        in_specs=vmem(len(weights) + PLANE) + [pl.BlockSpec(memory_space=pl.ANY)],
        out_specs=vmem(PLANE),
        cost_estimate=cost(span),
        compiler_params=pltpu.CompilerParams(vmem_limit_bytes=32 << 20),
        name="plane_product",
    )(*weights, cot, *firsts, after)
    return list(outs)


def unpack_kernel(columns, planes, axis, factor, offsets, *refs):
    pieces, out, buffer, sem = refs[:PLANE], refs[-3], refs[-2], refs[-1]
    me = lax.axis_index(axis)
    z, p = me // PLANE, me % PLANE
    copies = []
    for inner, offset in enumerate(offsets):
        block = lax.rem(z + planes + offset, planes)
        for k in range(PLANE):
            i = inner * PLANE + k
            span = slice(inner * columns, (inner + 1) * columns)
            if k == 0:
                source = pieces[k].at[:, span]
            else:
                buffer[i] = decode(pieces[k][:, span]) * factor
                source = buffer.at[i]
            start = pl.multiple_of((block * PLANE + (p ^ k)) * columns, 128)
            copy = pltpu.make_async_copy(source, out.at[:, pl.ds(start, columns)], sem.at[i])
            copy.start()
            copies.append(copy)
    for copy in copies:
        copy.wait()


def unpack(pieces, out, after, offsets, columns, planes, factor, span):
    rows = pieces[0].shape[0]
    count = len(offsets) * PLANE
    others = [*out, *after]
    return pl.pallas_call(
        functools.partial(unpack_kernel, columns, planes, "fsdp", factor, offsets),
        out_shape=jax.ShapeDtypeStruct((rows, columns * planes * PLANE), jnp.float32),
        in_specs=vmem(PLANE) + [pl.BlockSpec(memory_space=pl.ANY)] * len(others),
        out_specs=pl.BlockSpec(memory_space=pl.ANY),
        scratch_shapes=[
            pltpu.VMEM((count, rows, columns), jnp.float32),
            pltpu.SemaphoreType.DMA((count,)),
        ],
        input_output_aliases={PLANE: 0} if out else {},
        cost_estimate=cost(span),
        compiler_params=pltpu.CompilerParams(vmem_limit_bytes=32 << 20),
        name="unpack",
    )(*pieces, *others)


def on_device(
    features,
    value_cotangent,
    value_weight,
    first_moment,
    second_moment,
    fragment_local,
    fragment_anchor,
    outer_momentum,
):
    size = lax.axis_size("fsdp")
    planes = size // PLANE
    columns = features.shape[1] // size
    tokens = features.shape[0] * size
    gradient_scale = power_below(tokens * 24.0 * 6.0)
    product_scale = power_below(value_cotangent.shape[1] * 6.0 * 0.25)

    ring = [(i, (i + PLANE) % size) for i in range(size)]

    def around(x):
        return lax.ppermute(x, "fsdp", ring)

    def back(x):
        return lax.ppermute(x, "fsdp", [(to, source) for source, to in ring])

    def across(x, k):
        return lax.ppermute(x, "fsdp", [(i, i ^ k) for i in range(size)])

    workers = lax.axis_size("worker")
    half = planes // 2
    distances = [half]
    for step in range(half - 1, 0, -1):
        distances += [step, -step]
    distances.append(0)
    coded, weight, cot, own, chunks = pack(features, value_cotangent, value_weight, columns, distances)
    firsts = [across(first, k + 1) for k, (first, _) in enumerate(chunks)]
    others = [across(rest, k + 1) for k, (_, rest) in enumerate(chunks)]

    difference = fragment_anchor - fragment_local[0]
    if workers == 2:
        partner_local = lax.ppermute(fragment_local, "worker", [(0, 1), (1, 0)])
        pseudo_sum = difference + (fragment_anchor - partner_local[0])
    else:
        pseudo_sum = lax.psum(difference, "worker")
    pseudo_mean = pseudo_sum / workers
    new_momentum = outer_mass * outer_momentum + pseudo_mean
    new_anchor = fragment_anchor - outer_rate * (pseudo_mean + outer_mass * new_momentum)

    behind, ahead = around(coded), back(coded)
    behind, firsts = lax.optimization_barrier((behind, firsts))
    weights, offsets = [weight, behind, ahead], [0, -1, 1]

    def partials(spread, others, rest, dtype, span):
        return plane_partial(spread, own, cot, firsts, others, rest, columns, gradient_scale, dtype, span)

    plus, minus = partials([(0, 0, half > 1)], [], [behind], WIRE, C_PARTIAL[0])[0], None
    early = plane_product(weights, cot, firsts, new_momentum, columns, product_scale, C_PRODUCT[0])
    early = [part if k == 0 else across(part, k) for k, part in enumerate(early)]
    late_weights, late_offsets = [], []
    for step in range(half - 1, 0, -1):
        plus = around(plus)
        late_weights.append(plus)
        late_offsets.append(step - half - 1)
        spread, rest = [(planes - 1 - 2 * step, 1, step > 1)], [plus]
        if step > 1:
            rest.append(plus)
        if minus is None:
            carried = ahead
            spread.append((planes - 2 * step, 0, step > 1))
        else:
            carried = minus = back(minus)
            late_weights.append(minus)
            late_offsets.append(half - step)
            spread.append((planes - 2 * step, 1, step > 1))
            rest.append(minus)
        if step > 1:
            rest.append(carried)
        if step == half - 1:
            pass
        plus, minus = partials(spread, others, rest, WIRE, C_PARTIAL[1])
    factor = 1.0 / product_scale
    late = plane_product(late_weights, cot, firsts, plus, columns, product_scale, C_PRODUCT[1])
    for k in range(1, PLANE):
        late[k], early[k] = lax.optimization_barrier((late[k], early[k]))
        late[k] = across(late[k], k)
    feature_grad = unpack(early, [], [], offsets, columns, planes, factor, C_UNPACK[0])
    so_far = [around(plus), back(minus)]
    so_far[0], feature_grad = lax.optimization_barrier((so_far[0], feature_grad))
    (total,) = partials([(planes - 1, 2, False)], others, so_far, jnp.float32, C_PARTIAL[2])
    gradient = total * (1.0 / gradient_scale)

    first_new = first_decay * first_moment[0] + (1.0 - first_decay) * gradient
    second_new = second_decay * second_moment[0] + (1.0 - second_decay) * gradient * gradient
    first_hat = first_new / (1.0 - first_decay**adam_count)
    second_hat = second_new / (1.0 - second_decay**adam_count)
    weight_new = weight - inner_rate * (
        first_hat / (jnp.sqrt(second_hat) + adam_epsilon) + weight_decay * weight
    )
    feature_grad = unpack(
        late, [feature_grad], [first_new], late_offsets, columns, planes, factor, C_UNPACK[1]
    )
    return (
        feature_grad,
        weight_new[None],
        first_new[None],
        second_new[None],
        new_anchor,
        new_momentum,
    )


def solution(mesh):
    placed = (
        P(("worker", "fsdp"), None),
        P(("worker", "fsdp"), None),
        P("worker", "fsdp", None),
        P("worker", "fsdp", None),
        P("worker", "fsdp", None),
        P("worker", "fsdp", None),
        P("fsdp", None),
        P("fsdp", None),
    )
    return jax.shard_map(
        on_device,
        mesh=mesh,
        in_specs=placed,
        out_specs=(
            P(("worker", "fsdp"), None),
            P("worker", "fsdp", None),
            P("worker", "fsdp", None),
            P("worker", "fsdp", None),
            P("fsdp", None),
            P("fsdp", None),
        ),
        check_vma=False,
    )
```

```python
import functools

import jax
import jax.numpy as jnp
from jax import lax
from jax.experimental import pallas as pl
from jax.experimental.pallas import tpu as pltpu
from jax.sharding import PartitionSpec as P

first_decay = 0.9
second_decay = 0.95
inner_rate = 0.001
weight_decay = 0.1
adam_epsilon = 1e-08
adam_count = 10.0
outer_rate = 0.7
outer_mass = 0.9

PLANE = 4
WEIGHT_SCALE = 2.0**17
WIRE = jnp.bfloat16
ORDER = (3, 1, 2)
C_PARTIAL, C_PRODUCT, C_UNPACK = (33, 34, 20), (33, 20), (36, 30)


def cost(log_flops):
    return pl.CostEstimate(flops=1 << log_flops, bytes_accessed=1 << 20, transcendentals=0)


def power_below(limit):
    scale = 1.0
    while scale * limit > 32768.0:
        scale /= 2.0
    while scale * limit < 16384.0:
        scale *= 2.0
    return scale


def encode(x):
    power = x * x
    power = power * power
    power = power * power
    return jnp.where(x < 0.0, -power, power).astype(WIRE)


def decode(code):
    wide = code.astype(jnp.float32)
    size = jnp.abs(wide)
    root = jnp.where(size > 0.0, jnp.exp(jnp.log(size) * 0.125), 0.0)
    return jnp.where(wide < 0.0, -root, root)


def vmem(count):
    return [pl.BlockSpec(memory_space=pltpu.VMEM)] * count


def contract(left, right, dims):
    return lax.dot_general(left, right, (dims, ((), ())), preferred_element_type=jnp.float32)


def pack_kernel(columns, distances, axis, features_far, cot_in, weight_far, coded, weight, cot, own, *refs):
    chunks, (features, sem) = refs[:-2], refs[-2:]
    me = lax.axis_index(axis)
    z, p, planes = me // PLANE, me % PLANE, len(distances)
    copies = [
        pltpu.make_async_copy(weight_far.at[0], weight, sem.at[0]),
        pltpu.make_async_copy(features_far, features, sem.at[1]),
    ]
    for copy in copies:
        copy.start()
    cot[...] = cot_in[...]
    copies[0].wait()
    coded[...] = encode(weight[...] * WEIGHT_SCALE)
    copies[1].wait()
    for k in range(PLANE):
        if k > 0:
            first, middle, last = chunks[3 * k - 3 : 3 * k]
            first[:, : cot.shape[1]] = cot[...]
        for at, distance in enumerate(distances):
            block = lax.rem(z + planes + distance, planes)
            start = pl.multiple_of((block * PLANE + (p ^ k)) * columns, 128)
            value = features[:, pl.ds(start, columns)]
            if k == 0:
                own[:, at * columns : (at + 1) * columns] = value
            elif at == 0:
                first[:, cot.shape[1] :] = value
            elif at == planes - 1:
                last[...] = value
            else:
                middle[:, (at - 1) * columns : at * columns] = value


def pack(features, cot, weight, columns, distances):
    rows, planes = features.shape[0], len(distances)
    widths = [planes * columns] + [cot.shape[1] + columns, (planes - 2) * columns, columns] * (PLANE - 1)
    coded, weight, cot, own, *chunks = pl.pallas_call(
        functools.partial(pack_kernel, columns, distances, "fsdp"),
        out_shape=[
            jax.ShapeDtypeStruct(weight.shape[1:], WIRE),
            jax.ShapeDtypeStruct(weight.shape[1:], weight.dtype),
            jax.ShapeDtypeStruct(cot.shape, cot.dtype),
        ]
        + [jax.ShapeDtypeStruct((rows, width), features.dtype) for width in widths],
        in_specs=[pl.BlockSpec(memory_space=pltpu.HBM), *vmem(1), pl.BlockSpec(memory_space=pltpu.HBM)],
        out_specs=vmem(3 + len(widths)),
        scratch_shapes=[pltpu.VMEM(features.shape, features.dtype), pltpu.SemaphoreType.DMA((2,))],
        cost_estimate=cost(36),
        compiler_params=pltpu.CompilerParams(vmem_limit_bytes=48 << 20),
        name="pack",
    )(features, cot, weight)
    return coded, weight, cot, own, [chunks[k::3] for k in range(3)]


def partial_kernel(columns, scale, spread, own, cot, *refs):
    firsts, parts = refs[: PLANE - 1], refs[PLANE - 1 : 2 * PLANE - 2]
    rest, outs = refs[2 * PLANE - 2 : -len(spread)], refs[-len(spread) :]
    depth = cot.shape[1]
    for (at, start, count, rides), out in zip(spread, outs):
        total = contract(own[:, at : at + columns], cot[...], ((0,), (0,)))
        for part, first in zip(parts, firsts):
            total += contract(part[:, start : start + columns], first[:, :depth], ((0,), (0,)))
        total = total * scale
        for ref in rest[:count]:
            total += decode(ref[:columns, :])
        out[:columns, :] = encode(total) if out.dtype == WIRE else total
        if rides:
            out[columns:, :] = rest[count][-columns:, :]
        rest = rest[count + rides :]


def plane_partial(spread, own, cot, firsts, parts, rest, columns, scale, dtype, span):
    operands = [own, cot, *firsts, *parts, *rest]
    outs = pl.pallas_call(
        functools.partial(partial_kernel, columns, scale, spread),
        out_shape=[
            jax.ShapeDtypeStruct((columns * (1 + rides), cot.shape[1]), dtype) for *_, rides in spread
        ],
        in_specs=vmem(len(operands)),
        out_specs=vmem(len(spread)),
        cost_estimate=cost(span),
        compiler_params=pltpu.CompilerParams(vmem_limit_bytes=32 << 20),
        name="plane_partial",
    )(*operands)
    return list(outs)


def product_kernel(columns, count, scale, *refs):
    weights, cot, firsts, outs = refs[:count], refs[count], refs[count + 1 : count + PLANE], refs[-PLANE:]
    for rider, out in zip(refs[count + PLANE : -PLANE - 1], outs[1:]):
        out[:, count * columns :] = rider[...]
    depth = cot.shape[1]
    for i, weight in enumerate(weights):
        if weight.dtype == WIRE:
            wide, factor = decode(weight[-columns:, :]), 1.0 / WEIGHT_SCALE
        else:
            wide, factor = weight[...], 1.0
        high = wide.astype(jnp.bfloat16)
        low = (wide - high.astype(jnp.float32)).astype(jnp.bfloat16)
        for k in range(PLANE):
            rows = cot[...] if k == 0 else firsts[k - 1][:, :depth]
            result = contract(rows, high, ((1,), (1,))) + contract(rows, low, ((1,), (1,)))
            result = result * factor if k == 0 else encode(result * (factor * scale))
            outs[k][:, i * columns : (i + 1) * columns] = result


def plane_product(weights, cot, firsts, riders, after, columns, scale, span):
    rows, width = cot.shape[0], columns * len(weights)
    sizes = [width] + [width + (columns if riders else 0)] * (PLANE - 1)
    outs = pl.pallas_call(
        functools.partial(product_kernel, columns, len(weights), scale),
        out_shape=[
            jax.ShapeDtypeStruct((rows, size), jnp.float32 if k == 0 else WIRE) for k, size in enumerate(sizes)
        ],
        in_specs=vmem(len(weights) + PLANE + len(riders)) + [pl.BlockSpec(memory_space=pl.ANY)],
        out_specs=vmem(PLANE),
        cost_estimate=cost(span),
        compiler_params=pltpu.CompilerParams(vmem_limit_bytes=32 << 20),
        name="plane_product",
    )(*weights, cot, *firsts, *riders, after)
    return list(outs)


def unpack_kernel(columns, planes, axis, factor, offsets, *refs):
    pieces, out, buffer, sem = refs[:PLANE], refs[-3], refs[-2], refs[-1]
    me = lax.axis_index(axis)
    z, p = me // PLANE, me % PLANE
    copies = []
    for inner, offset in enumerate(offsets):
        block = lax.rem(z + planes + offset, planes)
        for k in range(PLANE):
            i = inner * PLANE + k
            span = slice(inner * columns, (inner + 1) * columns)
            if k == 0:
                source = pieces[k].at[:, span]
            else:
                buffer[i] = decode(pieces[k][:, span]) * factor
                source = buffer.at[i]
            start = pl.multiple_of((block * PLANE + (p ^ k)) * columns, 128)
            copy = pltpu.make_async_copy(source, out.at[:, pl.ds(start, columns)], sem.at[i])
            copy.start()
            copies.append(copy)
    for copy in copies:
        copy.wait()


def unpack(pieces, out, after, offsets, columns, planes, factor, span):
    rows = pieces[0].shape[0]
    count = len(offsets) * PLANE
    others = [*out, *after]
    return pl.pallas_call(
        functools.partial(unpack_kernel, columns, planes, "fsdp", factor, offsets),
        out_shape=jax.ShapeDtypeStruct((rows, columns * planes * PLANE), jnp.float32),
        in_specs=vmem(PLANE) + [pl.BlockSpec(memory_space=pl.ANY)] * len(others),
        out_specs=pl.BlockSpec(memory_space=pl.ANY),
        scratch_shapes=[
            pltpu.VMEM((count, rows, columns), jnp.float32),
            pltpu.SemaphoreType.DMA((count,)),
        ],
        input_output_aliases={PLANE: 0} if out else {},
        cost_estimate=cost(span),
        compiler_params=pltpu.CompilerParams(vmem_limit_bytes=32 << 20),
        name="unpack",
    )(*pieces, *others)


def on_device(
    features,
    value_cotangent,
    value_weight,
    first_moment,
    second_moment,
    fragment_local,
    fragment_anchor,
    outer_momentum,
):
    size = lax.axis_size("fsdp")
    planes = size // PLANE
    columns = features.shape[1] // size
    tokens = features.shape[0] * size
    gradient_scale = power_below(tokens * 24.0 * 6.0)
    product_scale = power_below(value_cotangent.shape[1] * 6.0 * 0.25)

    ring = [(i, (i + PLANE) % size) for i in range(size)]

    def around(x):
        return lax.ppermute(x, "fsdp", ring)

    def back(x):
        return lax.ppermute(x, "fsdp", [(to, source) for source, to in ring])

    def across(x, k):
        return lax.ppermute(x, "fsdp", [(i, i ^ k) for i in range(size)])

    def across_all(parts):
        moved = {k: across(parts[k - 1], k) for k in ORDER}
        return [moved[k] for k in range(1, PLANE)]

    workers = lax.axis_size("worker")
    half = planes // 2
    distances = [half]
    for step in range(half - 1, 0, -1):
        distances += [step, -step]
    distances.append(0)
    coded, weight, cot, own, chunks = pack(features, value_cotangent, value_weight, columns, distances)
    firsts, middles, riders = chunks
    firsts = across_all(firsts)
    middles = across_all(middles)

    difference = fragment_anchor - fragment_local[0]
    if workers == 2:
        partner_local = lax.ppermute(fragment_local, "worker", [(0, 1), (1, 0)])
        pseudo_sum = difference + (fragment_anchor - partner_local[0])
    else:
        pseudo_sum = lax.psum(difference, "worker")
    pseudo_mean = pseudo_sum / workers
    new_momentum = outer_mass * outer_momentum + pseudo_mean
    new_anchor = fragment_anchor - outer_rate * (pseudo_mean + outer_mass * new_momentum)

    behind, ahead = around(coded), back(coded)
    behind, firsts = lax.optimization_barrier((behind, firsts))
    weights, offsets = [weight, behind, ahead], [0, -1, 1]

    def partials(spread, parts, rest, dtype, span):
        return plane_partial(spread, own, cot, firsts, parts, rest, columns, gradient_scale, dtype, span)

    plus, minus = partials([(0, cot.shape[1], 0, half > 1)], firsts, [behind], WIRE, C_PARTIAL[0])[0], None
    early = plane_product(weights, cot, firsts, riders, new_momentum, columns, product_scale, C_PRODUCT[0])
    early[1:] = across_all(early[1:])
    late_weights, late_offsets = [], []
    for step in range(half - 1, 0, -1):
        plus = around(plus)
        late_weights.append(plus)
        late_offsets.append(step - half - 1)
        at = (planes - 1 - 2 * step) * columns
        spread, rest = [(at, at - columns, 1, step > 1)], [plus]
        if step > 1:
            rest.append(plus)
        if minus is None:
            carried = ahead
            spread.append((at + columns, at, 0, step > 1))
        else:
            carried = minus = back(minus)
            late_weights.append(minus)
            late_offsets.append(half - step)
            spread.append((at + columns, at, 1, step > 1))
            rest.append(minus)
        if step > 1:
            rest.append(carried)
        plus, minus = partials(spread, middles, rest, WIRE, C_PARTIAL[1])
    factor = 1.0 / product_scale
    late = plane_product(late_weights, cot, firsts, [], plus, columns, product_scale, C_PRODUCT[1])
    for k in range(1, PLANE):
        late[k], early[k] = lax.optimization_barrier((late[k], early[k]))
    late[1:] = across_all(late[1:])
    feature_grad = unpack(early, [], [], offsets, columns, planes, factor, C_UNPACK[0])
    so_far = [around(plus), back(minus)]
    so_far[0], feature_grad = lax.optimization_barrier((so_far[0], feature_grad))
    (total,) = partials(
        [((planes - 1) * columns, len(weights) * columns, 2, False)], early[1:], so_far, jnp.float32, C_PARTIAL[2])
    gradient = total * (1.0 / gradient_scale)

    first_new = first_decay * first_moment[0] + (1.0 - first_decay) * gradient
    second_new = second_decay * second_moment[0] + (1.0 - second_decay) * gradient * gradient
    first_hat = first_new / (1.0 - first_decay**adam_count)
    second_hat = second_new / (1.0 - second_decay**adam_count)
    weight_new = weight - inner_rate * (
        first_hat / (jnp.sqrt(second_hat) + adam_epsilon) + weight_decay * weight
    )
    feature_grad = unpack(
        late, [feature_grad], [first_new], late_offsets, columns, planes, factor, C_UNPACK[1]
    )
    return (
        feature_grad,
        weight_new[None],
        first_new[None],
        second_new[None],
        new_anchor,
        new_momentum,
    )


def solution(mesh):
    placed = (
        P(("worker", "fsdp"), None),
        P(("worker", "fsdp"), None),
        P("worker", "fsdp", None),
        P("worker", "fsdp", None),
        P("worker", "fsdp", None),
        P("worker", "fsdp", None),
        P("fsdp", None),
        P("fsdp", None),
    )
    return jax.shard_map(
        on_device,
        mesh=mesh,
        in_specs=placed,
        out_specs=(
            P(("worker", "fsdp"), None),
            P("worker", "fsdp", None),
            P("worker", "fsdp", None),
            P("worker", "fsdp", None),
            P("fsdp", None),
            P("fsdp", None),
        ),
        check_vma=False,
    )
```

```python
import functools

import jax
import jax.numpy as jnp
from jax import lax
from jax.experimental import pallas as pl
from jax.experimental.pallas import tpu as pltpu
from jax.sharding import PartitionSpec as P

first_decay = 0.9
second_decay = 0.95
inner_rate = 0.001
weight_decay = 0.1
adam_epsilon = 1e-08
adam_count = 10.0
outer_rate = 0.7
outer_mass = 0.9

PLANE = 4
WEIGHT_SCALE = 2.0**17
WIRE = jnp.bfloat16
ORDER = (1, 2, 3)
C_PARTIAL, C_PRODUCT, C_UNPACK = (36, 32, 34), (36, 20), (32, 20)


def cost(log_flops):
    return pl.CostEstimate(flops=1 << log_flops, bytes_accessed=1 << 20, transcendentals=0)


def power_below(limit):
    scale = 1.0
    while scale * limit > 32768.0:
        scale /= 2.0
    while scale * limit < 16384.0:
        scale *= 2.0
    return scale


def encode(x):
    power = x * x
    power = power * power
    power = power * power
    return jnp.where(x < 0.0, -power, power).astype(WIRE)


def decode(code):
    wide = code.astype(jnp.float32)
    size = jnp.abs(wide)
    root = jnp.where(size > 0.0, jnp.exp(jnp.log(size) * 0.125), 0.0)
    return jnp.where(wide < 0.0, -root, root)


def vmem(count):
    return [pl.BlockSpec(memory_space=pltpu.VMEM)] * count


def contract(left, right, dims):
    return lax.dot_general(left, right, (dims, ((), ())), preferred_element_type=jnp.float32)


def pack_kernel(columns, distances, axis, features_far, cot_in, weight_far, coded, weight, cot, own, *refs):
    chunks, (features, sem) = refs[:-2], refs[-2:]
    me = lax.axis_index(axis)
    z, p, planes = me // PLANE, me % PLANE, len(distances)
    copies = [
        pltpu.make_async_copy(weight_far.at[0], weight, sem.at[0]),
        pltpu.make_async_copy(features_far, features, sem.at[1]),
    ]
    for copy in copies:
        copy.start()
    cot[...] = cot_in[...]
    copies[0].wait()
    coded[...] = encode(weight[...] * WEIGHT_SCALE)
    copies[1].wait()
    for k in range(PLANE):
        if k > 0:
            first, middle, last = chunks[3 * k - 3 : 3 * k]
            first[:, : cot.shape[1]] = cot[...]
        for at, distance in enumerate(distances):
            block = lax.rem(z + planes + distance, planes)
            start = pl.multiple_of((block * PLANE + (p ^ k)) * columns, 128)
            value = features[:, pl.ds(start, columns)]
            if k == 0:
                own[:, at * columns : (at + 1) * columns] = value
            elif at == 0:
                first[:, cot.shape[1] :] = value
            elif at == planes - 1:
                last[...] = value
            else:
                middle[:, (at - 1) * columns : at * columns] = value


def pack(features, cot, weight, columns, distances):
    rows, planes = features.shape[0], len(distances)
    widths = [planes * columns] + [cot.shape[1] + columns, (planes - 2) * columns, columns] * (PLANE - 1)
    coded, weight, cot, own, *chunks = pl.pallas_call(
        functools.partial(pack_kernel, columns, distances, "fsdp"),
        out_shape=[
            jax.ShapeDtypeStruct(weight.shape[1:], WIRE),
            jax.ShapeDtypeStruct(weight.shape[1:], weight.dtype),
            jax.ShapeDtypeStruct(cot.shape, cot.dtype),
        ]
        + [jax.ShapeDtypeStruct((rows, width), features.dtype) for width in widths],
        in_specs=[pl.BlockSpec(memory_space=pltpu.HBM), *vmem(1), pl.BlockSpec(memory_space=pltpu.HBM)],
        out_specs=vmem(3 + len(widths)),
        scratch_shapes=[pltpu.VMEM(features.shape, features.dtype), pltpu.SemaphoreType.DMA((2,))],
        cost_estimate=cost(36),
        compiler_params=pltpu.CompilerParams(vmem_limit_bytes=48 << 20),
        name="pack",
    )(features, cot, weight)
    return coded, weight, cot, own, [chunks[k::3] for k in range(3)]


def partial_kernel(columns, scale, spread, own, cot, *refs):
    firsts, parts = refs[: PLANE - 1], refs[PLANE - 1 : 2 * PLANE - 2]
    rest, outs = refs[2 * PLANE - 2 : -len(spread)], refs[-len(spread) :]
    depth = cot.shape[1]
    for (at, start, count, rides), out in zip(spread, outs):
        total = contract(own[:, at : at + columns], cot[...], ((0,), (0,)))
        for part, first in zip(parts, firsts):
            total += contract(part[:, start : start + columns], first[:, :depth], ((0,), (0,)))
        total = total * scale
        for ref in rest[:count]:
            total += decode(ref[:columns, :])
        out[:columns, :] = encode(total) if out.dtype == WIRE else total
        if rides:
            out[columns:, :] = rest[count][-columns:, :]
        rest = rest[count + rides :]


def plane_partial(spread, own, cot, firsts, parts, rest, columns, scale, dtype, span):
    operands = [own, cot, *firsts, *parts, *rest]
    outs = pl.pallas_call(
        functools.partial(partial_kernel, columns, scale, spread),
        out_shape=[
            jax.ShapeDtypeStruct((columns * (1 + rides), cot.shape[1]), dtype) for *_, rides in spread
        ],
        in_specs=vmem(len(operands)),
        out_specs=vmem(len(spread)),
        cost_estimate=cost(span),
        compiler_params=pltpu.CompilerParams(vmem_limit_bytes=32 << 20),
        name="plane_partial",
    )(*operands)
    return list(outs)


def product_kernel(columns, count, scale, *refs):
    weights, cot, firsts, outs = refs[:count], refs[count], refs[count + 1 : count + PLANE], refs[-PLANE:]
    for rider, out in zip(refs[count + PLANE : -PLANE - 1], outs[1:]):
        out[:, count * columns :] = rider[...]
    depth = cot.shape[1]
    for i, weight in enumerate(weights):
        if weight.dtype == WIRE:
            wide, factor = decode(weight[-columns:, :]), 1.0 / WEIGHT_SCALE
        else:
            wide, factor = weight[...], 1.0
        high = wide.astype(jnp.bfloat16)
        low = (wide - high.astype(jnp.float32)).astype(jnp.bfloat16)
        for k in range(PLANE):
            rows = cot[...] if k == 0 else firsts[k - 1][:, :depth]
            result = contract(rows, high, ((1,), (1,))) + contract(rows, low, ((1,), (1,)))
            result = result * factor if k == 0 else encode(result * (factor * scale))
            outs[k][:, i * columns : (i + 1) * columns] = result


def plane_product(weights, cot, firsts, riders, after, columns, scale, span):
    rows, width = cot.shape[0], columns * len(weights)
    sizes = [width] + [width + (columns if riders else 0)] * (PLANE - 1)
    outs = pl.pallas_call(
        functools.partial(product_kernel, columns, len(weights), scale),
        out_shape=[
            jax.ShapeDtypeStruct((rows, size), jnp.float32 if k == 0 else WIRE) for k, size in enumerate(sizes)
        ],
        in_specs=vmem(len(weights) + PLANE + len(riders)) + [pl.BlockSpec(memory_space=pl.ANY)],
        out_specs=vmem(PLANE),
        cost_estimate=cost(span),
        compiler_params=pltpu.CompilerParams(vmem_limit_bytes=32 << 20),
        name="plane_product",
    )(*weights, cot, *firsts, *riders, after)
    return list(outs)


def unpack_kernel(columns, planes, axis, factor, offsets, *refs):
    pieces, out, buffer, sem = refs[:PLANE], refs[-3], refs[-2], refs[-1]
    me = lax.axis_index(axis)
    z, p = me // PLANE, me % PLANE
    copies = []
    for inner, offset in enumerate(offsets):
        block = lax.rem(z + planes + offset, planes)
        for k in range(PLANE):
            i = inner * PLANE + k
            span = slice(inner * columns, (inner + 1) * columns)
            if k == 0:
                source = pieces[k].at[:, span]
            else:
                buffer[i] = decode(pieces[k][:, span]) * factor
                source = buffer.at[i]
            start = pl.multiple_of((block * PLANE + (p ^ k)) * columns, 128)
            copy = pltpu.make_async_copy(source, out.at[:, pl.ds(start, columns)], sem.at[i])
            copy.start()
            copies.append(copy)
    for copy in copies:
        copy.wait()


def unpack(pieces, out, after, offsets, columns, planes, factor, span):
    rows = pieces[0].shape[0]
    count = len(offsets) * PLANE
    others = [*out, *after]
    return pl.pallas_call(
        functools.partial(unpack_kernel, columns, planes, "fsdp", factor, offsets),
        out_shape=jax.ShapeDtypeStruct((rows, columns * planes * PLANE), jnp.float32),
        in_specs=vmem(PLANE) + [pl.BlockSpec(memory_space=pl.ANY)] * len(others),
        out_specs=pl.BlockSpec(memory_space=pl.ANY),
        scratch_shapes=[
            pltpu.VMEM((count, rows, columns), jnp.float32),
            pltpu.SemaphoreType.DMA((count,)),
        ],
        input_output_aliases={PLANE: 0} if out else {},
        cost_estimate=cost(span),
        compiler_params=pltpu.CompilerParams(vmem_limit_bytes=32 << 20),
        name="unpack",
    )(*pieces, *others)


def on_device(
    features,
    value_cotangent,
    value_weight,
    first_moment,
    second_moment,
    fragment_local,
    fragment_anchor,
    outer_momentum,
):
    size = lax.axis_size("fsdp")
    planes = size // PLANE
    columns = features.shape[1] // size
    tokens = features.shape[0] * size
    gradient_scale = power_below(tokens * 24.0 * 6.0)
    product_scale = power_below(value_cotangent.shape[1] * 6.0 * 0.25)

    ring = [(i, (i + PLANE) % size) for i in range(size)]

    def around(x):
        return lax.ppermute(x, "fsdp", ring)

    def back(x):
        return lax.ppermute(x, "fsdp", [(to, source) for source, to in ring])

    def across(x, k):
        return lax.ppermute(x, "fsdp", [(i, i ^ k) for i in range(size)])

    def across_all(parts):
        moved = {k: across(parts[k - 1], k) for k in ORDER}
        return [moved[k] for k in range(1, PLANE)]

    workers = lax.axis_size("worker")
    half = planes // 2
    distances = [half]
    for step in range(half - 1, 0, -1):
        distances += [step, -step]
    distances.append(0)
    coded, weight, cot, own, chunks = pack(features, value_cotangent, value_weight, columns, distances)
    firsts, middles, riders = chunks
    if workers == 2:
        partner_local = lax.ppermute(fragment_local, "worker", [(0, 1), (1, 0)])
        firsts[-1], partner_local = lax.optimization_barrier((firsts[-1], partner_local))
    firsts = across_all(firsts)
    middles = across_all(middles)

    difference = fragment_anchor - fragment_local[0]
    if workers == 2:
        pseudo_sum = difference + (fragment_anchor - partner_local[0])
    else:
        pseudo_sum = lax.psum(difference, "worker")
    pseudo_mean = pseudo_sum / workers
    new_momentum = outer_mass * outer_momentum + pseudo_mean
    new_anchor = fragment_anchor - outer_rate * (pseudo_mean + outer_mass * new_momentum)

    behind, ahead = around(coded), back(coded)
    behind, firsts = lax.optimization_barrier((behind, firsts))
    weights, offsets = [weight, behind, ahead], [0, -1, 1]

    def partials(spread, parts, rest, dtype, span):
        return plane_partial(spread, own, cot, firsts, parts, rest, columns, gradient_scale, dtype, span)

    plus, minus = partials([(0, cot.shape[1], 0, half > 1)], firsts, [behind], WIRE, C_PARTIAL[0])[0], None
    early = plane_product(weights, cot, firsts, riders, new_momentum, columns, product_scale, C_PRODUCT[0])
    early[1:] = across_all(early[1:])
    late_weights, late_offsets = [], []
    for step in range(half - 1, 0, -1):
        plus = around(plus)
        late_weights.append(plus)
        late_offsets.append(step - half - 1)
        at = (planes - 1 - 2 * step) * columns
        spread, rest = [(at, at - columns, 1, step > 1)], [plus]
        if step > 1:
            rest.append(plus)
        if minus is None:
            carried = ahead
            spread.append((at + columns, at, 0, step > 1))
        else:
            carried = minus = back(minus)
            late_weights.append(minus)
            late_offsets.append(half - step)
            spread.append((at + columns, at, 1, step > 1))
            rest.append(minus)
        if step > 1:
            rest.append(carried)
        plus, minus = partials(spread, middles, rest, WIRE, C_PARTIAL[1])
    factor = 1.0 / product_scale
    late = plane_product(late_weights, cot, firsts, [], plus, columns, product_scale, C_PRODUCT[1])
    for k in range(1, PLANE):
        late[k], early[k] = lax.optimization_barrier((late[k], early[k]))
    late[1:] = across_all(late[1:])
    feature_grad = unpack(early, [], [], offsets, columns, planes, factor, C_UNPACK[0])
    so_far = [around(plus), back(minus)]
    so_far[0], feature_grad = lax.optimization_barrier((so_far[0], feature_grad))
    (total,) = partials(
        [((planes - 1) * columns, len(weights) * columns, 2, False)], early[1:], so_far, jnp.float32, C_PARTIAL[2])
    gradient = total * (1.0 / gradient_scale)

    first_new = first_decay * first_moment[0] + (1.0 - first_decay) * gradient
    second_new = second_decay * second_moment[0] + (1.0 - second_decay) * gradient * gradient
    first_hat = first_new / (1.0 - first_decay**adam_count)
    second_hat = second_new / (1.0 - second_decay**adam_count)
    weight_new = weight - inner_rate * (
        first_hat / (jnp.sqrt(second_hat) + adam_epsilon) + weight_decay * weight
    )
    feature_grad = unpack(
        late, [feature_grad], [first_new], late_offsets, columns, planes, factor, C_UNPACK[1]
    )
    return (
        feature_grad,
        weight_new[None],
        first_new[None],
        second_new[None],
        new_anchor,
        new_momentum,
    )


def solution(mesh):
    placed = (
        P(("worker", "fsdp"), None),
        P(("worker", "fsdp"), None),
        P("worker", "fsdp", None),
        P("worker", "fsdp", None),
        P("worker", "fsdp", None),
        P("worker", "fsdp", None),
        P("fsdp", None),
        P("fsdp", None),
    )
    return jax.shard_map(
        on_device,
        mesh=mesh,
        in_specs=placed,
        out_specs=(
            P(("worker", "fsdp"), None),
            P("worker", "fsdp", None),
            P("worker", "fsdp", None),
            P("worker", "fsdp", None),
            P("fsdp", None),
            P("fsdp", None),
        ),
        check_vma=False,
    )
```

```python
import functools

import jax
import jax.numpy as jnp
from jax import lax
from jax.experimental import pallas as pl
from jax.experimental.pallas import tpu as pltpu
from jax.sharding import PartitionSpec as P

first_decay = 0.9
second_decay = 0.95
inner_rate = 0.001
weight_decay = 0.1
adam_epsilon = 1e-08
adam_count = 10.0
outer_rate = 0.7
outer_mass = 0.9

PLANE = 4
WEIGHT_SCALE = 2.0**17
WIRE = jnp.bfloat16
PEERS = (0, 2, 3, 1)
C_PARTIAL, C_PRODUCT, C_UNPACK = (32, 32, 36), (33, 20), (36, 20)


def cost(log_flops):
    return pl.CostEstimate(flops=1 << log_flops, bytes_accessed=1 << 20, transcendentals=0)


def power_below(limit):
    scale = 1.0
    while scale * limit > 32768.0:
        scale /= 2.0
    while scale * limit < 16384.0:
        scale *= 2.0
    return scale


def encode(x):
    power = x * x
    power = power * power
    power = power * power
    return jnp.where(x < 0.0, -power, power).astype(WIRE)


def decode(code):
    wide = code.astype(jnp.float32)
    size = jnp.abs(wide)
    root = jnp.where(size > 0.0, jnp.exp(jnp.log(size) * 0.125), 0.0)
    return jnp.where(wide < 0.0, -root, root)


def vmem(count):
    return [pl.BlockSpec(memory_space=pltpu.VMEM)] * count


def contract(left, right, dims):
    return lax.dot_general(left, right, (dims, ((), ())), preferred_element_type=jnp.float32)


def pack_kernel(columns, distances, axis, features_far, cot_in, weight_far, coded, weight, cot, own, *refs):
    chunks, (features, sem) = refs[:-2], refs[-2:]
    me = lax.axis_index(axis)
    z, p, planes = me // PLANE, me % PLANE, len(distances)
    copies = [
        pltpu.make_async_copy(weight_far.at[0], weight, sem.at[0]),
        pltpu.make_async_copy(features_far, features, sem.at[1]),
    ]
    for copy in copies:
        copy.start()
    cot[...] = cot_in[...]
    copies[0].wait()
    coded[...] = encode(weight[...] * WEIGHT_SCALE)
    copies[1].wait()
    for k in range(PLANE):
        if k > 0:
            first, middle, last = chunks[3 * k - 3 : 3 * k]
            first[:, : cot.shape[1]] = cot[...]
        for at, distance in enumerate(distances):
            block = lax.rem(z + planes + distance, planes)
            start = pl.multiple_of((block * PLANE + (p ^ PEERS[k])) * columns, 128)
            value = features[:, pl.ds(start, columns)]
            if k == 0:
                own[:, at * columns : (at + 1) * columns] = value
            elif at == 0:
                first[:, cot.shape[1] :] = value
            elif at == planes - 1:
                last[...] = value
            else:
                middle[:, (at - 1) * columns : at * columns] = value


def pack(features, cot, weight, columns, distances):
    rows, planes = features.shape[0], len(distances)
    widths = [planes * columns] + [cot.shape[1] + columns, (planes - 2) * columns, columns] * (PLANE - 1)
    coded, weight, cot, own, *chunks = pl.pallas_call(
        functools.partial(pack_kernel, columns, distances, "fsdp"),
        out_shape=[
            jax.ShapeDtypeStruct(weight.shape[1:], WIRE),
            jax.ShapeDtypeStruct(weight.shape[1:], weight.dtype),
            jax.ShapeDtypeStruct(cot.shape, cot.dtype),
        ]
        + [jax.ShapeDtypeStruct((rows, width), features.dtype) for width in widths],
        in_specs=[pl.BlockSpec(memory_space=pltpu.HBM), *vmem(1), pl.BlockSpec(memory_space=pltpu.HBM)],
        out_specs=vmem(3 + len(widths)),
        scratch_shapes=[pltpu.VMEM(features.shape, features.dtype), pltpu.SemaphoreType.DMA((2,))],
        cost_estimate=cost(36),
        compiler_params=pltpu.CompilerParams(vmem_limit_bytes=48 << 20),
        name="pack",
    )(features, cot, weight)
    return coded, weight, cot, own, [chunks[k::3] for k in range(3)]


def partial_kernel(columns, scale, spread, own, cot, *refs):
    firsts, parts = refs[: PLANE - 1], refs[PLANE - 1 : 2 * PLANE - 2]
    rest, outs = refs[2 * PLANE - 2 : -len(spread)], refs[-len(spread) :]
    depth = cot.shape[1]
    for (at, start, count, rides), out in zip(spread, outs):
        total = contract(own[:, at : at + columns], cot[...], ((0,), (0,)))
        for part, first in zip(parts, firsts):
            total += contract(part[:, start : start + columns], first[:, :depth], ((0,), (0,)))
        total = total * scale
        for ref in rest[:count]:
            total += decode(ref[:columns, :])
        out[:columns, :] = encode(total) if out.dtype == WIRE else total
        if rides:
            out[columns:, :] = rest[count][-columns:, :]
        rest = rest[count + rides :]


def plane_partial(spread, own, cot, firsts, parts, rest, columns, scale, dtype, span):
    operands = [own, cot, *firsts, *parts, *rest]
    outs = pl.pallas_call(
        functools.partial(partial_kernel, columns, scale, spread),
        out_shape=[
            jax.ShapeDtypeStruct((columns * (1 + rides), cot.shape[1]), dtype) for *_, rides in spread
        ],
        in_specs=vmem(len(operands)),
        out_specs=vmem(len(spread)),
        cost_estimate=cost(span),
        compiler_params=pltpu.CompilerParams(vmem_limit_bytes=32 << 20),
        name="plane_partial",
    )(*operands)
    return list(outs)


def product_kernel(columns, count, scale, *refs):
    weights, cot, firsts, outs = refs[:count], refs[count], refs[count + 1 : count + PLANE], refs[-PLANE:]
    for rider, out in zip(refs[count + PLANE : -PLANE - 1], outs[1:]):
        out[:, count * columns :] = rider[...]
    depth = cot.shape[1]
    for i, weight in enumerate(weights):
        if weight.dtype == WIRE:
            wide, factor = decode(weight[-columns:, :]), 1.0 / WEIGHT_SCALE
        else:
            wide, factor = weight[...], 1.0
        high = wide.astype(jnp.bfloat16)
        low = (wide - high.astype(jnp.float32)).astype(jnp.bfloat16)
        for k in range(PLANE):
            rows = cot[...] if k == 0 else firsts[k - 1][:, :depth]
            result = contract(rows, high, ((1,), (1,))) + contract(rows, low, ((1,), (1,)))
            result = result * factor if k == 0 else encode(result * (factor * scale))
            outs[k][:, i * columns : (i + 1) * columns] = result


def plane_product(weights, cot, firsts, riders, after, columns, scale, span):
    rows, width = cot.shape[0], columns * len(weights)
    sizes = [width] + [width + (columns if riders else 0)] * (PLANE - 1)
    outs = pl.pallas_call(
        functools.partial(product_kernel, columns, len(weights), scale),
        out_shape=[
            jax.ShapeDtypeStruct((rows, size), jnp.float32 if k == 0 else WIRE) for k, size in enumerate(sizes)
        ],
        in_specs=vmem(len(weights) + PLANE + len(riders)) + [pl.BlockSpec(memory_space=pl.ANY)],
        out_specs=vmem(PLANE),
        cost_estimate=cost(span),
        compiler_params=pltpu.CompilerParams(vmem_limit_bytes=32 << 20),
        name="plane_product",
    )(*weights, cot, *firsts, *riders, after)
    return list(outs)


def unpack_kernel(columns, planes, axis, factor, offsets, *refs):
    pieces, out, buffer, sem = refs[:PLANE], refs[-3], refs[-2], refs[-1]
    me = lax.axis_index(axis)
    z, p = me // PLANE, me % PLANE
    copies = []
    for inner, offset in enumerate(offsets):
        block = lax.rem(z + planes + offset, planes)
        for k in range(PLANE):
            i = inner * PLANE + k
            span = slice(inner * columns, (inner + 1) * columns)
            if k == 0:
                source = pieces[k].at[:, span]
            else:
                buffer[i] = decode(pieces[k][:, span]) * factor
                source = buffer.at[i]
            start = pl.multiple_of((block * PLANE + (p ^ PEERS[k])) * columns, 128)
            copy = pltpu.make_async_copy(source, out.at[:, pl.ds(start, columns)], sem.at[i])
            copy.start()
            copies.append(copy)
    for copy in copies:
        copy.wait()


def unpack(pieces, out, after, offsets, columns, planes, factor, span):
    rows = pieces[0].shape[0]
    count = len(offsets) * PLANE
    others = [*out, *after]
    return pl.pallas_call(
        functools.partial(unpack_kernel, columns, planes, "fsdp", factor, offsets),
        out_shape=jax.ShapeDtypeStruct((rows, columns * planes * PLANE), jnp.float32),
        in_specs=vmem(PLANE) + [pl.BlockSpec(memory_space=pl.ANY)] * len(others),
        out_specs=pl.BlockSpec(memory_space=pl.ANY),
        scratch_shapes=[
            pltpu.VMEM((count, rows, columns), jnp.float32),
            pltpu.SemaphoreType.DMA((count,)),
        ],
        input_output_aliases={PLANE: 0} if out else {},
        cost_estimate=cost(span),
        compiler_params=pltpu.CompilerParams(vmem_limit_bytes=32 << 20),
        name="unpack",
    )(*pieces, *others)


def on_device(
    features,
    value_cotangent,
    value_weight,
    first_moment,
    second_moment,
    fragment_local,
    fragment_anchor,
    outer_momentum,
):
    size = lax.axis_size("fsdp")
    planes = size // PLANE
    columns = features.shape[1] // size
    tokens = features.shape[0] * size
    gradient_scale = power_below(tokens * 24.0 * 6.0)
    product_scale = power_below(value_cotangent.shape[1] * 6.0 * 0.25)

    ring = [(i, (i + PLANE) % size) for i in range(size)]

    def around(x):
        return lax.ppermute(x, "fsdp", ring)

    def back(x):
        return lax.ppermute(x, "fsdp", [(to, source) for source, to in ring])

    def across(x, k):
        return lax.ppermute(x, "fsdp", [(i, i ^ PEERS[k]) for i in range(size)])

    def across_all(parts):
        return [across(part, k + 1) for k, part in enumerate(parts)]

    workers = lax.axis_size("worker")
    half = planes // 2
    distances = [half]
    for step in range(half - 1, 0, -1):
        distances += [step, -step]
    distances.append(0)
    coded, weight, cot, own, chunks = pack(features, value_cotangent, value_weight, columns, distances)
    firsts, middles, riders = chunks
    if workers == 2:
        partner_local = lax.ppermute(fragment_local, "worker", [(0, 1), (1, 0)])
        firsts[-1], partner_local = lax.optimization_barrier((firsts[-1], partner_local))
    firsts = across_all(firsts)
    middles = across_all(middles)

    difference = fragment_anchor - fragment_local[0]
    if workers == 2:
        pseudo_sum = difference + (fragment_anchor - partner_local[0])
    else:
        pseudo_sum = lax.psum(difference, "worker")
    pseudo_mean = pseudo_sum / workers
    new_momentum = outer_mass * outer_momentum + pseudo_mean
    new_anchor = fragment_anchor - outer_rate * (pseudo_mean + outer_mass * new_momentum)

    behind, ahead = around(coded), back(coded)
    behind, firsts = lax.optimization_barrier((behind, firsts))
    weights, offsets = [weight, behind, ahead], [0, -1, 1]

    def partials(spread, parts, rest, dtype, span):
        return plane_partial(spread, own, cot, firsts, parts, rest, columns, gradient_scale, dtype, span)

    plus, minus = partials([(0, cot.shape[1], 0, False)], firsts, [], WIRE, C_PARTIAL[0])[0], None
    early = plane_product(weights, cot, firsts, riders, new_momentum, columns, product_scale, C_PRODUCT[0])
    early[1:] = across_all(early[1:])
    late_weights, late_offsets = [], []
    for step in range(half - 1, 0, -1):
        plus = around(plus)
        if step == half - 1:
            behind, plus = lax.optimization_barrier((behind, plus))
        behind = around(behind)
        late_weights.append(behind)
        late_offsets.append(step - half - 1)
        at = (planes - 1 - 2 * step) * columns
        spread, rest = [(at, at - columns, 1, False), (at + columns, at, 0, False)], [plus]
        if minus is not None:
            minus, ahead = back(minus), back(ahead)
            late_weights.append(ahead)
            late_offsets.append(half - step)
            spread[1] = (at + columns, at, 1, False)
            rest.append(minus)
        plus, minus = partials(spread, middles, rest, WIRE, C_PARTIAL[1])
    factor = 1.0 / product_scale
    late = plane_product(late_weights, cot, firsts, [], plus, columns, product_scale, C_PRODUCT[1])
    for k in range(1, PLANE):
        late[k], early[k] = lax.optimization_barrier((late[k], early[k]))
    late[1:] = across_all(late[1:])
    feature_grad = unpack(early, [], [], offsets, columns, planes, factor, C_UNPACK[0])
    so_far = [around(plus), back(minus)]
    so_far[0], feature_grad = lax.optimization_barrier((so_far[0], feature_grad))
    (total,) = partials(
        [((planes - 1) * columns, len(weights) * columns, 2, False)], early[1:], so_far, jnp.float32, C_PARTIAL[2])
    gradient = total * (1.0 / gradient_scale)

    first_new = first_decay * first_moment[0] + (1.0 - first_decay) * gradient
    second_new = second_decay * second_moment[0] + (1.0 - second_decay) * gradient * gradient
    first_hat = first_new / (1.0 - first_decay**adam_count)
    second_hat = second_new / (1.0 - second_decay**adam_count)
    weight_new = weight - inner_rate * (
        first_hat / (jnp.sqrt(second_hat) + adam_epsilon) + weight_decay * weight
    )
    feature_grad = unpack(
        late, [feature_grad], [first_new], late_offsets, columns, planes, factor, C_UNPACK[1]
    )
    return (
        feature_grad,
        weight_new[None],
        first_new[None],
        second_new[None],
        new_anchor,
        new_momentum,
    )


def solution(mesh):
    placed = (
        P(("worker", "fsdp"), None),
        P(("worker", "fsdp"), None),
        P("worker", "fsdp", None),
        P("worker", "fsdp", None),
        P("worker", "fsdp", None),
        P("worker", "fsdp", None),
        P("fsdp", None),
        P("fsdp", None),
    )
    return jax.shard_map(
        on_device,
        mesh=mesh,
        in_specs=placed,
        out_specs=(
            P(("worker", "fsdp"), None),
            P("worker", "fsdp", None),
            P("worker", "fsdp", None),
            P("worker", "fsdp", None),
            P("fsdp", None),
            P("fsdp", None),
        ),
        check_vma=False,
    )
```

```python
import functools

import jax
import jax.numpy as jnp
from jax import lax
from jax.experimental import pallas as pl
from jax.experimental.pallas import tpu as pltpu
from jax.sharding import PartitionSpec as P

first_decay = 0.9
second_decay = 0.95
inner_rate = 0.001
weight_decay = 0.1
adam_epsilon = 1e-08
adam_count = 10.0
outer_rate = 0.7
outer_mass = 0.9

PLANE = 4
WEIGHT_SCALE = 2.0**17
WIRE = jnp.bfloat16
PEERS = (0, 2, 3, 1)
C_PARTIAL, C_PRODUCT, C_UNPACK = (32, 33, 34), (36, 34), (33, 20)


def cost(log_flops):
    return pl.CostEstimate(flops=1 << log_flops, bytes_accessed=1 << 20, transcendentals=0)


def power_below(limit):
    scale = 1.0
    while scale * limit > 32768.0:
        scale /= 2.0
    while scale * limit < 16384.0:
        scale *= 2.0
    return scale


def encode(x):
    power = x * x
    power = power * power
    power = power * power
    return jnp.where(x < 0.0, -power, power).astype(WIRE)


def decode(code):
    wide = code.astype(jnp.float32)
    size = jnp.abs(wide)
    root = jnp.where(size > 0.0, jnp.exp(jnp.log(size) * 0.125), 0.0)
    return jnp.where(wide < 0.0, -root, root)


def vmem(count):
    return [pl.BlockSpec(memory_space=pltpu.VMEM)] * count


def contract(left, right, dims):
    return lax.dot_general(left, right, (dims, ((), ())), preferred_element_type=jnp.float32)


def pack_kernel(columns, distances, axis, features_far, cot_in, weight_far, coded, weight, cot, own, *refs):
    chunks, (features, sem) = refs[:-2], refs[-2:]
    me = lax.axis_index(axis)
    z, p, planes = me // PLANE, me % PLANE, len(distances)
    copies = [
        pltpu.make_async_copy(weight_far.at[0], weight, sem.at[0]),
        pltpu.make_async_copy(features_far, features, sem.at[1]),
    ]
    for copy in copies:
        copy.start()
    cot[...] = cot_in[...]
    copies[0].wait()
    coded[...] = encode(weight[...] * WEIGHT_SCALE)
    copies[1].wait()
    for k in range(PLANE):
        if k > 0:
            first, middle, last = chunks[3 * k - 3 : 3 * k]
        for at, distance in enumerate(distances):
            block = lax.rem(z + planes + distance, planes)
            start = pl.multiple_of((block * PLANE + (p ^ PEERS[k])) * columns, 128)
            value = features[:, pl.ds(start, columns)]
            if k == 0:
                own[:, at * columns : (at + 1) * columns] = value
            elif at == 0:
                first[...] = value
            elif at == planes - 1:
                last[...] = value
            else:
                middle[:, (at - 1) * columns : at * columns] = value


def pack(features, cot, weight, columns, distances):
    rows, planes = features.shape[0], len(distances)
    widths = [planes * columns] + [columns, (planes - 2) * columns, columns] * (PLANE - 1)
    coded, weight, cot, own, *chunks = pl.pallas_call(
        functools.partial(pack_kernel, columns, distances, "fsdp"),
        out_shape=[
            jax.ShapeDtypeStruct(weight.shape[1:], WIRE),
            jax.ShapeDtypeStruct(weight.shape[1:], weight.dtype),
            jax.ShapeDtypeStruct(cot.shape, cot.dtype),
        ]
        + [jax.ShapeDtypeStruct((rows, width), features.dtype) for width in widths],
        in_specs=[pl.BlockSpec(memory_space=pltpu.HBM), *vmem(1), pl.BlockSpec(memory_space=pltpu.HBM)],
        out_specs=vmem(3 + len(widths)),
        scratch_shapes=[pltpu.VMEM(features.shape, features.dtype), pltpu.SemaphoreType.DMA((2,))],
        cost_estimate=cost(36),
        compiler_params=pltpu.CompilerParams(vmem_limit_bytes=48 << 20),
        name="pack",
    )(features, cot, weight)
    return coded, weight, cot, own, [chunks[k::3] for k in range(3)]


def partial_kernel(columns, scale, spread, own, *refs):
    cots, parts = refs[:PLANE], refs[PLANE : 2 * PLANE - 1]
    rest, outs = refs[2 * PLANE - 1 : -len(spread)], refs[-len(spread) :]
    for (at, start, count, rides), out in zip(spread, outs):
        total = contract(own[:, at : at + columns], cots[0][...], ((0,), (0,)))
        for part, cot in zip(parts, cots[1:]):
            total += contract(part[:, start : start + columns], cot[...], ((0,), (0,)))
        total = total * scale
        for ref in rest[:count]:
            total += decode(ref[:columns, :])
        out[:columns, :] = encode(total) if out.dtype == WIRE else total
        if rides:
            out[columns:, :] = rest[count][-columns:, :]
        rest = rest[count + rides :]


def plane_partial(spread, own, cots, parts, rest, columns, scale, dtype, span):
    operands = [own, *cots, *parts, *rest]
    outs = pl.pallas_call(
        functools.partial(partial_kernel, columns, scale, spread),
        out_shape=[
            jax.ShapeDtypeStruct((columns * (1 + rides), cots[0].shape[1]), dtype) for *_, rides in spread
        ],
        in_specs=vmem(len(operands)),
        out_specs=vmem(len(spread)),
        cost_estimate=cost(span),
        compiler_params=pltpu.CompilerParams(vmem_limit_bytes=32 << 20),
        name="plane_partial",
    )(*operands)
    return list(outs)


def product_kernel(columns, count, scale, *refs):
    weights, cots, outs = refs[:count], refs[count : count + PLANE], refs[-PLANE:]
    for rider, out in zip(refs[count + PLANE : -PLANE - 1], outs[1:]):
        out[:, count * columns :] = rider[...]
    for i, weight in enumerate(weights):
        if weight.dtype == WIRE:
            wide, factor = decode(weight[-columns:, :]), 1.0 / WEIGHT_SCALE
        else:
            wide, factor = weight[...], 1.0
        high = wide.astype(jnp.bfloat16)
        low = (wide - high.astype(jnp.float32)).astype(jnp.bfloat16)
        for k in range(PLANE):
            rows = cots[k][...]
            result = contract(rows, high, ((1,), (1,))) + contract(rows, low, ((1,), (1,)))
            result = result * factor if k == 0 else encode(result * (factor * scale))
            outs[k][:, i * columns : (i + 1) * columns] = result


def plane_product(weights, cots, riders, after, columns, scale, span):
    rows, width = cots[0].shape[0], columns * len(weights)
    sizes = [width] + [width + (columns if riders else 0)] * (PLANE - 1)
    outs = pl.pallas_call(
        functools.partial(product_kernel, columns, len(weights), scale),
        out_shape=[
            jax.ShapeDtypeStruct((rows, size), jnp.float32 if k == 0 else WIRE) for k, size in enumerate(sizes)
        ],
        in_specs=vmem(len(weights) + PLANE + len(riders)) + [pl.BlockSpec(memory_space=pl.ANY)],
        out_specs=vmem(PLANE),
        cost_estimate=cost(span),
        compiler_params=pltpu.CompilerParams(vmem_limit_bytes=32 << 20),
        name="plane_product",
    )(*weights, *cots, *riders, after)
    return list(outs)


def unpack_kernel(columns, planes, axis, factor, offsets, *refs):
    pieces, out, buffer, sem = refs[:PLANE], refs[-3], refs[-2], refs[-1]
    me = lax.axis_index(axis)
    z, p = me // PLANE, me % PLANE
    copies = []
    for inner, offset in enumerate(offsets):
        block = lax.rem(z + planes + offset, planes)
        for k in range(PLANE):
            i = inner * PLANE + k
            span = slice(inner * columns, (inner + 1) * columns)
            if k == 0:
                source = pieces[k].at[:, span]
            else:
                buffer[i] = decode(pieces[k][:, span]) * factor
                source = buffer.at[i]
            start = pl.multiple_of((block * PLANE + (p ^ PEERS[k])) * columns, 128)
            copy = pltpu.make_async_copy(source, out.at[:, pl.ds(start, columns)], sem.at[i])
            copy.start()
            copies.append(copy)
    for copy in copies:
        copy.wait()


def unpack(pieces, out, after, offsets, columns, planes, factor, span):
    rows = pieces[0].shape[0]
    count = len(offsets) * PLANE
    others = [*out, *after]
    return pl.pallas_call(
        functools.partial(unpack_kernel, columns, planes, "fsdp", factor, offsets),
        out_shape=jax.ShapeDtypeStruct((rows, columns * planes * PLANE), jnp.float32),
        in_specs=vmem(PLANE) + [pl.BlockSpec(memory_space=pl.ANY)] * len(others),
        out_specs=pl.BlockSpec(memory_space=pl.ANY),
        scratch_shapes=[
            pltpu.VMEM((count, rows, columns), jnp.float32),
            pltpu.SemaphoreType.DMA((count,)),
        ],
        input_output_aliases={PLANE: 0} if out else {},
        cost_estimate=cost(span),
        compiler_params=pltpu.CompilerParams(vmem_limit_bytes=32 << 20),
        name="unpack",
    )(*pieces, *others)


def on_device(
    features,
    value_cotangent,
    value_weight,
    first_moment,
    second_moment,
    fragment_local,
    fragment_anchor,
    outer_momentum,
):
    size = lax.axis_size("fsdp")
    planes = size // PLANE
    columns = features.shape[1] // size
    tokens = features.shape[0] * size
    gradient_scale = power_below(tokens * 24.0 * 6.0)
    product_scale = power_below(value_cotangent.shape[1] * 6.0 * 0.25)

    ring = [(i, (i + PLANE) % size) for i in range(size)]

    def around(x):
        return lax.ppermute(x, "fsdp", ring)

    def back(x):
        return lax.ppermute(x, "fsdp", [(to, source) for source, to in ring])

    def across(x, k):
        return lax.ppermute(x, "fsdp", [(i, i ^ PEERS[k]) for i in range(size)])

    def across_all(parts):
        return [across(part, k + 1) for k, part in enumerate(parts)]

    workers = lax.axis_size("worker")
    half = planes // 2
    distances = [half]
    for step in range(half - 1, 0, -1):
        distances += [step, -step]
    distances.append(0)
    coded, weight, cot, own, chunks = pack(features, value_cotangent, value_weight, columns, distances)
    firsts, middles, riders = chunks
    if workers == 2:
        partner_local = lax.ppermute(fragment_local, "worker", [(0, 1), (1, 0)])
        coded, partner_local = lax.optimization_barrier((coded, partner_local))
    by_y = across(cot, 1)
    by_x = across(cot, 3)
    cots = [cot, by_y, across(by_y, 3), by_x]
    firsts = across_all(firsts)
    middles = across_all(middles)

    difference = fragment_anchor - fragment_local[0]
    if workers == 2:
        pseudo_sum = difference + (fragment_anchor - partner_local[0])
    else:
        pseudo_sum = lax.psum(difference, "worker")
    pseudo_mean = pseudo_sum / workers
    new_momentum = outer_mass * outer_momentum + pseudo_mean
    new_anchor = fragment_anchor - outer_rate * (pseudo_mean + outer_mass * new_momentum)

    behind, ahead = around(coded), back(coded)
    behind, firsts = lax.optimization_barrier((behind, firsts))
    weights, offsets = [weight, behind, ahead], [0, -1, 1]

    def partials(spread, parts, rest, dtype, span):
        return plane_partial(spread, own, cots, parts, rest, columns, gradient_scale, dtype, span)

    plus, minus = partials([(0, 0, 0, half > 1)], firsts, [behind], WIRE, C_PARTIAL[0])[0], None
    early = plane_product(weights, cots, riders, new_momentum, columns, product_scale, C_PRODUCT[0])
    early[1:] = across_all(early[1:])
    late_weights, late_offsets = [], []
    for step in range(half - 1, 0, -1):
        plus = around(plus)
        late_weights.append(plus)
        late_offsets.append(step - half - 1)
        at = (planes - 1 - 2 * step) * columns
        spread, rest = [(at, at - columns, 1, step > 1)], [plus]
        if step > 1:
            rest.append(plus)
        if minus is None:
            carried = ahead
            spread.append((at + columns, at, 0, step > 1))
        else:
            carried = minus = back(minus)
            late_weights.append(minus)
            late_offsets.append(half - step)
            spread.append((at + columns, at, 1, step > 1))
            rest.append(minus)
        if step > 1:
            rest.append(carried)
        plus, minus = partials(spread, middles, rest, WIRE, C_PARTIAL[1])
    factor = 1.0 / product_scale
    late = plane_product(late_weights, cots, [], plus, columns, product_scale, C_PRODUCT[1])
    for k in range(1, PLANE):
        late[k], early[k] = lax.optimization_barrier((late[k], early[k]))
    late[1:] = across_all(late[1:])
    feature_grad = unpack(early, [], [], offsets, columns, planes, factor, C_UNPACK[0])
    so_far = [around(plus), back(minus)]
    so_far[0], feature_grad = lax.optimization_barrier((so_far[0], feature_grad))
    (total,) = partials(
        [((planes - 1) * columns, len(weights) * columns, 2, False)], early[1:], so_far, jnp.float32, C_PARTIAL[2])
    gradient = total * (1.0 / gradient_scale)

    first_new = first_decay * first_moment[0] + (1.0 - first_decay) * gradient
    second_new = second_decay * second_moment[0] + (1.0 - second_decay) * gradient * gradient
    first_hat = first_new / (1.0 - first_decay**adam_count)
    second_hat = second_new / (1.0 - second_decay**adam_count)
    weight_new = weight - inner_rate * (
        first_hat / (jnp.sqrt(second_hat) + adam_epsilon) + weight_decay * weight
    )
    feature_grad = unpack(
        late, [feature_grad], [first_new], late_offsets, columns, planes, factor, C_UNPACK[1]
    )
    return (
        feature_grad,
        weight_new[None],
        first_new[None],
        second_new[None],
        new_anchor,
        new_momentum,
    )


def solution(mesh):
    placed = (
        P(("worker", "fsdp"), None),
        P(("worker", "fsdp"), None),
        P("worker", "fsdp", None),
        P("worker", "fsdp", None),
        P("worker", "fsdp", None),
        P("worker", "fsdp", None),
        P("fsdp", None),
        P("fsdp", None),
    )
    return jax.shard_map(
        on_device,
        mesh=mesh,
        in_specs=placed,
        out_specs=(
            P(("worker", "fsdp"), None),
            P("worker", "fsdp", None),
            P("worker", "fsdp", None),
            P("worker", "fsdp", None),
            P("fsdp", None),
            P("fsdp", None),
        ),
        check_vma=False,
    )
```

```python
import functools

import jax
import jax.numpy as jnp
from jax import lax
from jax.experimental import pallas as pl
from jax.experimental.pallas import tpu as pltpu
from jax.sharding import PartitionSpec as P

first_decay = 0.9
second_decay = 0.95
inner_rate = 0.001
weight_decay = 0.1
adam_epsilon = 1e-08
adam_count = 10.0
outer_rate = 0.7
outer_mass = 0.9

PLANE = 4
WEIGHT_SCALE = 2.0**17
WIRE = jnp.bfloat16
PEERS = (0, 2, 3, 1)
C_PARTIAL, C_PRODUCT, C_UNPACK = (33, 34, 32), (33, 34), (32, 20)


def cost(log_flops):
    return pl.CostEstimate(flops=1 << log_flops, bytes_accessed=1 << 20, transcendentals=0)


def power_below(limit):
    scale = 1.0
    while scale * limit > 32768.0:
        scale /= 2.0
    while scale * limit < 16384.0:
        scale *= 2.0
    return scale


def encode(x):
    power = x * x
    power = power * power
    power = power * power
    return jnp.where(x < 0.0, -power, power).astype(WIRE)


def decode(code):
    wide = code.astype(jnp.float32)
    size = jnp.abs(wide)
    root = jnp.where(size > 0.0, jnp.exp(jnp.log(size) * 0.125), 0.0)
    return jnp.where(wide < 0.0, -root, root)


def vmem(count):
    return [pl.BlockSpec(memory_space=pltpu.VMEM)] * count


def contract(left, right, dims):
    return lax.dot_general(left, right, (dims, ((), ())), preferred_element_type=jnp.float32)


def pack_kernel(columns, distances, axis, features_far, cot_in, weight_far, coded, weight, cot, own, *refs):
    chunks, (features, sem) = refs[:-2], refs[-2:]
    me = lax.axis_index(axis)
    z, p, planes = me // PLANE, me % PLANE, len(distances)
    copies = [
        pltpu.make_async_copy(weight_far.at[0], weight, sem.at[0]),
        pltpu.make_async_copy(features_far, features, sem.at[1]),
    ]
    for copy in copies:
        copy.start()
    cot[...] = cot_in[...]
    copies[0].wait()
    coded[...] = encode(weight[...] * WEIGHT_SCALE)
    copies[1].wait()
    for k in range(PLANE):
        if k > 0:
            first, middle, last = chunks[3 * k - 3 : 3 * k]
        for at, distance in enumerate(distances):
            block = lax.rem(z + planes + distance, planes)
            start = pl.multiple_of((block * PLANE + (p ^ PEERS[k])) * columns, 128)
            value = features[:, pl.ds(start, columns)]
            if k == 0:
                own[:, at * columns : (at + 1) * columns] = value
            elif at == 0:
                first[...] = value
            elif at == planes - 1:
                last[...] = value
            else:
                middle[:, (at - 1) * columns : at * columns] = value


def pack(features, cot, weight, columns, distances):
    rows, planes = features.shape[0], len(distances)
    widths = [planes * columns] + [columns, (planes - 2) * columns, columns] * (PLANE - 1)
    coded, weight, cot, own, *chunks = pl.pallas_call(
        functools.partial(pack_kernel, columns, distances, "fsdp"),
        out_shape=[
            jax.ShapeDtypeStruct(weight.shape[1:], WIRE),
            jax.ShapeDtypeStruct(weight.shape[1:], weight.dtype),
            jax.ShapeDtypeStruct(cot.shape, cot.dtype),
        ]
        + [jax.ShapeDtypeStruct((rows, width), features.dtype) for width in widths],
        in_specs=[pl.BlockSpec(memory_space=pltpu.HBM), *vmem(1), pl.BlockSpec(memory_space=pltpu.HBM)],
        out_specs=vmem(3 + len(widths)),
        scratch_shapes=[pltpu.VMEM(features.shape, features.dtype), pltpu.SemaphoreType.DMA((2,))],
        cost_estimate=cost(36),
        compiler_params=pltpu.CompilerParams(vmem_limit_bytes=48 << 20),
        name="pack",
    )(features, cot, weight)
    return coded, weight, cot, own, [chunks[k::3] for k in range(3)]


def partial_kernel(columns, scale, spread, own, *refs):
    cots, parts = refs[:PLANE], refs[PLANE : 2 * PLANE - 1]
    rest, outs = refs[2 * PLANE - 1 : -len(spread)], refs[-len(spread) :]
    for (at, start, count, rides), out in zip(spread, outs):
        total = contract(own[:, at : at + columns], cots[0][...], ((0,), (0,)))
        for part, cot in zip(parts, cots[1:]):
            total += contract(part[:, start : start + columns], cot[...], ((0,), (0,)))
        total = total * scale
        for ref in rest[:count]:
            total += decode(ref[:columns, :])
        out[:columns, :] = encode(total) if out.dtype == WIRE else total
        if rides:
            out[columns:, :] = rest[count][-columns:, :]
        rest = rest[count + rides :]


def plane_partial(spread, own, cots, parts, rest, columns, scale, dtype, span):
    operands = [own, *cots, *parts, *rest]
    outs = pl.pallas_call(
        functools.partial(partial_kernel, columns, scale, spread),
        out_shape=[
            jax.ShapeDtypeStruct((columns * (1 + rides), cots[0].shape[1]), dtype) for *_, rides in spread
        ],
        in_specs=vmem(len(operands)),
        out_specs=vmem(len(spread)),
        cost_estimate=cost(span),
        compiler_params=pltpu.CompilerParams(vmem_limit_bytes=32 << 20),
        name="plane_partial",
    )(*operands)
    return list(outs)


def product_kernel(columns, count, scale, *refs):
    weights, cots, outs = refs[:count], refs[count : count + PLANE], refs[-PLANE:]
    for rider, out in zip(refs[count + PLANE : -PLANE - 1], outs[1:]):
        out[:, count * columns :] = rider[...]
    for i, weight in enumerate(weights):
        if weight.dtype == WIRE:
            wide, factor = decode(weight[-columns:, :]), 1.0 / WEIGHT_SCALE
        else:
            wide, factor = weight[...], 1.0
        high = wide.astype(jnp.bfloat16)
        low = (wide - high.astype(jnp.float32)).astype(jnp.bfloat16)
        for k in range(PLANE):
            rows = cots[k][...]
            result = contract(rows, high, ((1,), (1,))) + contract(rows, low, ((1,), (1,)))
            result = result * factor if k == 0 else encode(result * (factor * scale))
            outs[k][:, i * columns : (i + 1) * columns] = result


def plane_product(weights, cots, riders, after, columns, scale, span):
    rows, width = cots[0].shape[0], columns * len(weights)
    sizes = [width] + [width + (columns if riders else 0)] * (PLANE - 1)
    outs = pl.pallas_call(
        functools.partial(product_kernel, columns, len(weights), scale),
        out_shape=[
            jax.ShapeDtypeStruct((rows, size), jnp.float32 if k == 0 else WIRE) for k, size in enumerate(sizes)
        ],
        in_specs=vmem(len(weights) + PLANE + len(riders)) + [pl.BlockSpec(memory_space=pl.ANY)],
        out_specs=vmem(PLANE),
        cost_estimate=cost(span),
        compiler_params=pltpu.CompilerParams(vmem_limit_bytes=32 << 20),
        name="plane_product",
    )(*weights, *cots, *riders, after)
    return list(outs)


def unpack_kernel(columns, planes, axis, factor, offsets, *refs):
    pieces, out, buffer, sem = refs[:PLANE], refs[-3], refs[-2], refs[-1]
    me = lax.axis_index(axis)
    z, p = me // PLANE, me % PLANE
    copies = []
    for inner, offset in enumerate(offsets):
        block = lax.rem(z + planes + offset, planes)
        for k in range(PLANE):
            i = inner * PLANE + k
            span = slice(inner * columns, (inner + 1) * columns)
            if k == 0:
                source = pieces[k].at[:, span]
            else:
                buffer[i] = decode(pieces[k][:, span]) * factor
                source = buffer.at[i]
            start = pl.multiple_of((block * PLANE + (p ^ PEERS[k])) * columns, 128)
            copy = pltpu.make_async_copy(source, out.at[:, pl.ds(start, columns)], sem.at[i])
            copy.start()
            copies.append(copy)
    for copy in copies:
        copy.wait()


def unpack(pieces, out, after, offsets, columns, planes, factor, span):
    rows = pieces[0].shape[0]
    count = len(offsets) * PLANE
    others = [*out, *after]
    return pl.pallas_call(
        functools.partial(unpack_kernel, columns, planes, "fsdp", factor, offsets),
        out_shape=jax.ShapeDtypeStruct((rows, columns * planes * PLANE), jnp.float32),
        in_specs=vmem(PLANE) + [pl.BlockSpec(memory_space=pl.ANY)] * len(others),
        out_specs=pl.BlockSpec(memory_space=pl.ANY),
        scratch_shapes=[
            pltpu.VMEM((count, rows, columns), jnp.float32),
            pltpu.SemaphoreType.DMA((count,)),
        ],
        input_output_aliases={PLANE: 0} if out else {},
        cost_estimate=cost(span),
        compiler_params=pltpu.CompilerParams(vmem_limit_bytes=32 << 20),
        name="unpack",
    )(*pieces, *others)


def on_device(
    features,
    value_cotangent,
    value_weight,
    first_moment,
    second_moment,
    fragment_local,
    fragment_anchor,
    outer_momentum,
):
    size = lax.axis_size("fsdp")
    planes = size // PLANE
    columns = features.shape[1] // size
    tokens = features.shape[0] * size
    gradient_scale = power_below(tokens * 24.0 * 6.0)
    product_scale = power_below(value_cotangent.shape[1] * 6.0 * 0.25)

    ring = [(i, (i + PLANE) % size) for i in range(size)]

    def around(x):
        return lax.ppermute(x, "fsdp", ring)

    def back(x):
        return lax.ppermute(x, "fsdp", [(to, source) for source, to in ring])

    def across(x, k):
        return lax.ppermute(x, "fsdp", [(i, i ^ PEERS[k]) for i in range(size)])

    def across_all(parts):
        return [across(part, k + 1) for k, part in enumerate(parts)]

    workers = lax.axis_size("worker")
    half = planes // 2
    distances = [half]
    for step in range(half - 1, 0, -1):
        distances += [step, -step]
    distances.append(0)
    coded, weight, cot, own, chunks = pack(features, value_cotangent, value_weight, columns, distances)
    firsts, middles, riders = chunks
    if workers == 2:
        partner_local = lax.ppermute(fragment_local, "worker", [(0, 1), (1, 0)])
        coded, partner_local = lax.optimization_barrier((coded, partner_local))
    by_y = across(cot, 1)
    by_x = across(cot, 3)
    cots = [cot, by_y, across(by_y, 3), by_x]
    firsts = across_all(firsts)
    middles = across_all(middles)

    difference = fragment_anchor - fragment_local[0]
    if workers == 2:
        pseudo_sum = difference + (fragment_anchor - partner_local[0])
    else:
        pseudo_sum = lax.psum(difference, "worker")
    pseudo_mean = pseudo_sum / workers
    new_momentum = outer_mass * outer_momentum + pseudo_mean
    new_anchor = fragment_anchor - outer_rate * (pseudo_mean + outer_mass * new_momentum)

    behind, ahead = around(coded), back(coded)
    behind, ahead, firsts = lax.optimization_barrier((behind, ahead, firsts))
    weights, offsets = [weight, behind, ahead], [0, -1, 1]

    def partials(spread, parts, rest, dtype, span):
        return plane_partial(spread, own, cots, parts, rest, columns, gradient_scale, dtype, span)

    plus, minus = partials([(0, 0, 0, half > 1)], firsts, [behind], WIRE, C_PARTIAL[0])[0], None
    early = plane_product(weights, cots, riders, new_momentum, columns, product_scale, C_PRODUCT[0])
    early[1:] = across_all(early[1:])
    late_weights, late_offsets = [], []
    for step in range(half - 1, 0, -1):
        plus = around(plus)
        late_weights.append(plus)
        late_offsets.append(step - half - 1)
        at = (planes - 1 - 2 * step) * columns
        spread, rest = [(at, at - columns, 1, step > 1)], [plus]
        if step > 1:
            rest.append(plus)
        if minus is None:
            carried = ahead
            spread.append((at + columns, at, 0, step > 1))
        else:
            carried = minus = back(minus)
            late_weights.append(minus)
            late_offsets.append(half - step)
            spread.append((at + columns, at, 1, step > 1))
            rest.append(minus)
        if step > 1:
            rest.append(carried)
        plus, minus = partials(spread, middles, rest, WIRE, C_PARTIAL[1])
    factor = 1.0 / product_scale
    late = plane_product(late_weights, cots, [], plus, columns, product_scale, C_PRODUCT[1])
    for k in range(1, PLANE):
        late[k], early[k] = lax.optimization_barrier((late[k], early[k]))
    late[1:] = across_all(late[1:])
    feature_grad = unpack(early, [], [], offsets, columns, planes, factor, C_UNPACK[0])
    so_far = [around(plus), back(minus)]
    so_far[0], feature_grad = lax.optimization_barrier((so_far[0], feature_grad))
    (total,) = partials(
        [((planes - 1) * columns, len(weights) * columns, 2, False)], early[1:], so_far, jnp.float32, C_PARTIAL[2])
    gradient = total * (1.0 / gradient_scale)

    first_new = first_decay * first_moment[0] + (1.0 - first_decay) * gradient
    second_new = second_decay * second_moment[0] + (1.0 - second_decay) * gradient * gradient
    first_hat = first_new / (1.0 - first_decay**adam_count)
    second_hat = second_new / (1.0 - second_decay**adam_count)
    weight_new = weight - inner_rate * (
        first_hat / (jnp.sqrt(second_hat) + adam_epsilon) + weight_decay * weight
    )
    feature_grad = unpack(
        late, [feature_grad], [first_new], late_offsets, columns, planes, factor, C_UNPACK[1]
    )
    return (
        feature_grad,
        weight_new[None],
        first_new[None],
        second_new[None],
        new_anchor,
        new_momentum,
    )


def solution(mesh):
    placed = (
        P(("worker", "fsdp"), None),
        P(("worker", "fsdp"), None),
        P("worker", "fsdp", None),
        P("worker", "fsdp", None),
        P("worker", "fsdp", None),
        P("worker", "fsdp", None),
        P("fsdp", None),
        P("fsdp", None),
    )
    return jax.shard_map(
        on_device,
        mesh=mesh,
        in_specs=placed,
        out_specs=(
            P(("worker", "fsdp"), None),
            P("worker", "fsdp", None),
            P("worker", "fsdp", None),
            P("worker", "fsdp", None),
            P("fsdp", None),
            P("fsdp", None),
        ),
        check_vma=False,
    )
```

```python
import functools

import jax
import jax.numpy as jnp
from jax import lax
from jax.experimental import pallas as pl
from jax.experimental.pallas import tpu as pltpu
from jax.sharding import PartitionSpec as P

first_decay = 0.9
second_decay = 0.95
inner_rate = 0.001
weight_decay = 0.1
adam_epsilon = 1e-08
adam_count = 10.0
outer_rate = 0.7
outer_mass = 0.9

PLANE = 4
WEIGHT_SCALE = 2.0**17
WIRE = jnp.bfloat16
PEERS = (0, 2, 3, 1)
C_PARTIAL, C_PRODUCT, C_UNPACK = (33, 34, 20), (33, 20), (36, 30)


def cost(log_flops):
    return pl.CostEstimate(flops=1 << log_flops, bytes_accessed=1 << 20, transcendentals=0)


def power_below(limit):
    scale = 1.0
    while scale * limit > 32768.0:
        scale /= 2.0
    while scale * limit < 16384.0:
        scale *= 2.0
    return scale


def encode(x):
    power = x * x
    power = power * power
    power = power * power
    return jnp.where(x < 0.0, -power, power).astype(WIRE)


def decode(code):
    wide = code.astype(jnp.float32)
    size = jnp.abs(wide)
    root = jnp.where(size > 0.0, jnp.exp(jnp.log(size) * 0.125), 0.0)
    return jnp.where(wide < 0.0, -root, root)


def vmem(count):
    return [pl.BlockSpec(memory_space=pltpu.VMEM)] * count


def contract(left, right, dims):
    return lax.dot_general(left, right, (dims, ((), ())), preferred_element_type=jnp.float32)


def pack_kernel(columns, distances, axis, features_far, cot_in, weight_far, coded, weight, cot, own, *refs):
    chunks, (features, sem) = refs[:-2], refs[-2:]
    me = lax.axis_index(axis)
    z, p, planes = me // PLANE, me % PLANE, len(distances)
    copies = [
        pltpu.make_async_copy(weight_far.at[0], weight, sem.at[0]),
        pltpu.make_async_copy(features_far, features, sem.at[1]),
    ]
    for copy in copies:
        copy.start()
    cot[...] = cot_in[...]
    copies[0].wait()
    coded[...] = encode(weight[...] * WEIGHT_SCALE)
    copies[1].wait()
    for k in range(PLANE):
        if k > 0:
            first, middle, last = chunks[3 * k - 3 : 3 * k]
            first[:, : cot.shape[1]] = cot[...]
        for at, distance in enumerate(distances):
            block = lax.rem(z + planes + distance, planes)
            start = pl.multiple_of((block * PLANE + (p ^ PEERS[k])) * columns, 128)
            value = features[:, pl.ds(start, columns)]
            if k == 0:
                own[:, at * columns : (at + 1) * columns] = value
            elif at == 0:
                first[:, cot.shape[1] :] = value
            elif at == planes - 1:
                last[...] = value
            else:
                middle[:, (at - 1) * columns : at * columns] = value


def pack(features, cot, weight, columns, distances):
    rows, planes = features.shape[0], len(distances)
    widths = [planes * columns] + [cot.shape[1] + columns, (planes - 2) * columns, columns] * (PLANE - 1)
    coded, weight, cot, own, *chunks = pl.pallas_call(
        functools.partial(pack_kernel, columns, distances, "fsdp"),
        out_shape=[
            jax.ShapeDtypeStruct(weight.shape[1:], WIRE),
            jax.ShapeDtypeStruct(weight.shape[1:], weight.dtype),
            jax.ShapeDtypeStruct(cot.shape, cot.dtype),
        ]
        + [jax.ShapeDtypeStruct((rows, width), features.dtype) for width in widths],
        in_specs=[pl.BlockSpec(memory_space=pltpu.HBM), *vmem(1), pl.BlockSpec(memory_space=pltpu.HBM)],
        out_specs=vmem(3 + len(widths)),
        scratch_shapes=[pltpu.VMEM(features.shape, features.dtype), pltpu.SemaphoreType.DMA((2,))],
        cost_estimate=cost(36),
        compiler_params=pltpu.CompilerParams(vmem_limit_bytes=48 << 20),
        name="pack",
    )(features, cot, weight)
    return coded, weight, cot, own, [chunks[k::3] for k in range(3)]


def partial_kernel(columns, scale, spread, own, cot, *refs):
    firsts, parts = refs[: PLANE - 1], refs[PLANE - 1 : 2 * PLANE - 2]
    rest, outs = refs[2 * PLANE - 2 : -len(spread)], refs[-len(spread) :]
    depth = cot.shape[1]
    for (at, start, count, rides), out in zip(spread, outs):
        total = contract(own[:, at : at + columns], cot[...], ((0,), (0,)))
        for part, first in zip(parts, firsts):
            total += contract(part[:, start : start + columns], first[:, :depth], ((0,), (0,)))
        total = total * scale
        for ref in rest[:count]:
            total += decode(ref[:columns, :])
        out[:columns, :] = encode(total) if out.dtype == WIRE else total
        if rides:
            out[columns:, :] = rest[count][-columns:, :]
        rest = rest[count + rides :]


def plane_partial(spread, own, cot, firsts, parts, rest, columns, scale, dtype, span):
    operands = [own, cot, *firsts, *parts, *rest]
    outs = pl.pallas_call(
        functools.partial(partial_kernel, columns, scale, spread),
        out_shape=[
            jax.ShapeDtypeStruct((columns * (1 + rides), cot.shape[1]), dtype) for *_, rides in spread
        ],
        in_specs=vmem(len(operands)),
        out_specs=vmem(len(spread)),
        cost_estimate=cost(span),
        compiler_params=pltpu.CompilerParams(vmem_limit_bytes=32 << 20),
        name="plane_partial",
    )(*operands)
    return list(outs)


def product_kernel(columns, count, scale, *refs):
    weights, cot, firsts, outs = refs[:count], refs[count], refs[count + 1 : count + PLANE], refs[-PLANE:]
    for rider, out in zip(refs[count + PLANE : -PLANE - 1], outs[1:]):
        out[:, count * columns :] = rider[...]
    depth = cot.shape[1]
    for i, weight in enumerate(weights):
        if weight.dtype == WIRE:
            wide, factor = decode(weight[-columns:, :]), 1.0 / WEIGHT_SCALE
        else:
            wide, factor = weight[...], 1.0
        high = wide.astype(jnp.bfloat16)
        low = (wide - high.astype(jnp.float32)).astype(jnp.bfloat16)
        for k in range(PLANE):
            rows = cot[...] if k == 0 else firsts[k - 1][:, :depth]
            result = contract(rows, high, ((1,), (1,))) + contract(rows, low, ((1,), (1,)))
            result = result * factor if k == 0 else encode(result * (factor * scale))
            outs[k][:, i * columns : (i + 1) * columns] = result


def plane_product(weights, cot, firsts, riders, after, columns, scale, span):
    rows, width = cot.shape[0], columns * len(weights)
    sizes = [width] + [width + (columns if riders else 0)] * (PLANE - 1)
    outs = pl.pallas_call(
        functools.partial(product_kernel, columns, len(weights), scale),
        out_shape=[
            jax.ShapeDtypeStruct((rows, size), jnp.float32 if k == 0 else WIRE) for k, size in enumerate(sizes)
        ],
        in_specs=vmem(len(weights) + PLANE + len(riders)) + [pl.BlockSpec(memory_space=pl.ANY)],
        out_specs=vmem(PLANE),
        cost_estimate=cost(span),
        compiler_params=pltpu.CompilerParams(vmem_limit_bytes=32 << 20),
        name="plane_product",
    )(*weights, cot, *firsts, *riders, after)
    return list(outs)


def unpack_kernel(columns, planes, axis, factor, offsets, *refs):
    pieces, out, buffer, sem = refs[:PLANE], refs[-3], refs[-2], refs[-1]
    me = lax.axis_index(axis)
    z, p = me // PLANE, me % PLANE
    copies = []
    for inner, offset in enumerate(offsets):
        block = lax.rem(z + planes + offset, planes)
        for k in range(PLANE):
            i = inner * PLANE + k
            span = slice(inner * columns, (inner + 1) * columns)
            if k == 0:
                source = pieces[k].at[:, span]
            else:
                buffer[i] = decode(pieces[k][:, span]) * factor
                source = buffer.at[i]
            start = pl.multiple_of((block * PLANE + (p ^ PEERS[k])) * columns, 128)
            copy = pltpu.make_async_copy(source, out.at[:, pl.ds(start, columns)], sem.at[i])
            copy.start()
            copies.append(copy)
    for copy in copies:
        copy.wait()


def unpack(pieces, out, after, offsets, columns, planes, factor, span):
    rows = pieces[0].shape[0]
    count = len(offsets) * PLANE
    others = [*out, *after]
    return pl.pallas_call(
        functools.partial(unpack_kernel, columns, planes, "fsdp", factor, offsets),
        out_shape=jax.ShapeDtypeStruct((rows, columns * planes * PLANE), jnp.float32),
        in_specs=vmem(PLANE) + [pl.BlockSpec(memory_space=pl.ANY)] * len(others),
        out_specs=pl.BlockSpec(memory_space=pl.ANY),
        scratch_shapes=[
            pltpu.VMEM((count, rows, columns), jnp.float32),
            pltpu.SemaphoreType.DMA((count,)),
        ],
        input_output_aliases={PLANE: 0} if out else {},
        cost_estimate=cost(span),
        compiler_params=pltpu.CompilerParams(vmem_limit_bytes=32 << 20),
        name="unpack",
    )(*pieces, *others)


def on_device(
    features,
    value_cotangent,
    value_weight,
    first_moment,
    second_moment,
    fragment_local,
    fragment_anchor,
    outer_momentum,
):
    size = lax.axis_size("fsdp")
    planes = size // PLANE
    columns = features.shape[1] // size
    tokens = features.shape[0] * size
    gradient_scale = power_below(tokens * 24.0 * 6.0)
    product_scale = power_below(value_cotangent.shape[1] * 6.0 * 0.25)

    ring = [(i, (i + PLANE) % size) for i in range(size)]

    def around(x):
        return lax.ppermute(x, "fsdp", ring)

    def back(x):
        return lax.ppermute(x, "fsdp", [(to, source) for source, to in ring])

    def across(x, k):
        return lax.ppermute(x, "fsdp", [(i, i ^ PEERS[k]) for i in range(size)])

    def across_all(parts):
        return [across(part, k + 1) for k, part in enumerate(parts)]

    workers = lax.axis_size("worker")
    half = planes // 2
    distances = [half]
    for step in range(half - 1, 0, -1):
        distances += [step, -step]
    distances.append(0)
    coded, weight, cot, own, chunks = pack(features, value_cotangent, value_weight, columns, distances)
    firsts, middles, riders = chunks
    firsts = across_all(firsts)
    middles = across_all(middles)

    difference = fragment_anchor - fragment_local[0]
    if workers == 2:
        partner_local = lax.ppermute(fragment_local, "worker", [(0, 1), (1, 0)])
        pseudo_sum = difference + (fragment_anchor - partner_local[0])
    else:
        pseudo_sum = lax.psum(difference, "worker")
    pseudo_mean = pseudo_sum / workers
    new_momentum = outer_mass * outer_momentum + pseudo_mean
    new_anchor = fragment_anchor - outer_rate * (pseudo_mean + outer_mass * new_momentum)

    behind, ahead = around(coded), back(coded)
    behind, firsts = lax.optimization_barrier((behind, firsts))
    weights, offsets = [weight, behind, ahead], [0, -1, 1]

    def partials(spread, parts, rest, dtype, span):
        return plane_partial(spread, own, cot, firsts, parts, rest, columns, gradient_scale, dtype, span)

    plus, minus = partials([(0, cot.shape[1], 0, half > 1)], firsts, [behind], WIRE, C_PARTIAL[0])[0], None
    early = plane_product(weights, cot, firsts, riders, new_momentum, columns, product_scale, C_PRODUCT[0])
    early[1:] = across_all(early[1:])
    late_weights, late_offsets = [], []
    for step in range(half - 1, 0, -1):
        plus = around(plus)
        late_weights.append(plus)
        late_offsets.append(step - half - 1)
        at = (planes - 1 - 2 * step) * columns
        spread, rest = [(at, at - columns, 1, step > 1)], [plus]
        if step > 1:
            rest.append(plus)
        if minus is None:
            carried = ahead
            spread.append((at + columns, at, 0, step > 1))
        else:
            carried = minus = back(minus)
            late_weights.append(minus)
            late_offsets.append(half - step)
            spread.append((at + columns, at, 1, step > 1))
            rest.append(minus)
        if step > 1:
            rest.append(carried)
        plus, minus = partials(spread, middles, rest, WIRE, C_PARTIAL[1])
    factor = 1.0 / product_scale
    late = plane_product(late_weights, cot, firsts, [], plus, columns, product_scale, C_PRODUCT[1])
    for k in range(1, PLANE):
        late[k], early[k] = lax.optimization_barrier((late[k], early[k]))
    late[1:] = across_all(late[1:])
    feature_grad = unpack(early, [], [], offsets, columns, planes, factor, C_UNPACK[0])
    so_far = [around(plus), back(minus)]
    so_far[0], feature_grad = lax.optimization_barrier((so_far[0], feature_grad))
    (total,) = partials(
        [((planes - 1) * columns, len(weights) * columns, 2, False)], early[1:], so_far, jnp.float32, C_PARTIAL[2])
    gradient = total * (1.0 / gradient_scale)

    first_new = first_decay * first_moment[0] + (1.0 - first_decay) * gradient
    second_new = second_decay * second_moment[0] + (1.0 - second_decay) * gradient * gradient
    first_hat = first_new / (1.0 - first_decay**adam_count)
    second_hat = second_new / (1.0 - second_decay**adam_count)
    weight_new = weight - inner_rate * (
        first_hat / (jnp.sqrt(second_hat) + adam_epsilon) + weight_decay * weight
    )
    feature_grad = unpack(
        late, [feature_grad], [first_new], late_offsets, columns, planes, factor, C_UNPACK[1]
    )
    return (
        feature_grad,
        weight_new[None],
        first_new[None],
        second_new[None],
        new_anchor,
        new_momentum,
    )


def solution(mesh):
    placed = (
        P(("worker", "fsdp"), None),
        P(("worker", "fsdp"), None),
        P("worker", "fsdp", None),
        P("worker", "fsdp", None),
        P("worker", "fsdp", None),
        P("worker", "fsdp", None),
        P("fsdp", None),
        P("fsdp", None),
    )
    return jax.shard_map(
        on_device,
        mesh=mesh,
        in_specs=placed,
        out_specs=(
            P(("worker", "fsdp"), None),
            P("worker", "fsdp", None),
            P("worker", "fsdp", None),
            P("worker", "fsdp", None),
            P("fsdp", None),
            P("fsdp", None),
        ),
        check_vma=False,
    )
```
